256 devices in a mesh: row: 16 (over z, core), col: 16 (over x, y).
Axes of the slice: x: 4, y: 4, z: 8, core: 2. Of those that a mesh axis runs over, the one named last changes fastest.
Arguments:
- tokens: bfloat16 [2048, 3072], P('col', 'row'), may hold values from -6 to 6
- gate_weight: bfloat16 [3072, 8192], P('row', 'col'), may hold values from -0.109375 to 0.109375
- up_weight: bfloat16 [3072, 8192], P('row', 'col'), may hold values from -0.109375 to 0.109375
- down_weight: bfloat16 [8192, 3072], P('col', 'row'), may hold values from -0.0625 to 0.0625
- cotangent: bfloat16 [2048, 3072], P('col', 'row'), may hold values from -6 to 6
Outputs:
- output: bfloat16 [2048, 3072], P('col', 'row')
- grad_tokens: bfloat16 [2048, 3072], P('col', 'row')
- grad_gate: bfloat16 [3072, 8192], P('row', 'col')
- grad_up: bfloat16 [3072, 8192], P('row', 'col')
- grad_down: bfloat16 [8192, 3072], P('col', 'row')
The draws below stay inside these ranges and needn't reach their ends.
All inputs are finite; a program needn't handle non-finite values.
Results may differ from the reference program's by a relative error of at most 0.005.
Values may be sent and summed in bfloat16 or wider, within the bound.
A program may use at most 64 MiB of HBM per device.

```python
import jax
import jax.numpy as jnp
from jax import lax

D = 3072
FF = 8192
TOKENS = 2048


def levels(rng, extent, shards, smallest, largest):
    def one(axis_at, shards_of):
        steps = jax.random.uniform(jax.random.fold_in(jax.random.fold_in(rng, 6), axis_at), (shards_of,), jnp.float32, smallest / len(shards), largest / len(shards))
        return jnp.repeat(jnp.exp(steps), extent[axis_at] // shards_of).reshape((-1,) + (1,) * (len(extent) - axis_at - 1))

    level = one(*shards[0])
    for cut in shards[1:]:
        level = level * one(*cut)
    return level


def centred(stream_key, shape, spread, reach, pieces=(), dtype=jnp.bfloat16):
    entries = spread * jax.random.normal(stream_key, shape, jnp.float32)
    if pieces:
        entries = entries * levels(stream_key, shape, pieces, -0.22, 0.18)
    return jnp.clip(entries, -reach, reach).astype(dtype)


def setup_inputs(seed: int = 0) -> dict:
    splits = jax.random.split(jax.random.key(seed), 6)
    tokens = centred(splits[0], (TOKENS, D), 1.0, 6.0, ((0, 16), (1, 16)))
    gate_weight = centred(splits[1], (D, FF), D ** -0.5, 0.109375, ((0, 16), (1, 16)))
    up_weight = centred(splits[2], (D, FF), D ** -0.5, 0.109375, ((0, 16), (1, 16)))
    down_weight = centred(splits[3], (FF, D), FF ** -0.5, 0.0625, ((0, 16), (1, 16)))
    cotangent = centred(splits[4], (TOKENS, D), 1.0, 6.0, ((0, 16), (1, 16)))
    return {"tokens": tokens, "gate_weight": gate_weight, "up_weight": up_weight, "down_weight": down_weight, "cotangent": cotangent}


def reference(tokens, gate_weight, up_weight, down_weight, cotangent):
    gate = jnp.dot(tokens, gate_weight, preferred_element_type=jnp.float32)
    up = jnp.dot(tokens, up_weight, preferred_element_type=jnp.float32)
    sigma = jax.nn.sigmoid(gate)
    silu_gate = gate * sigma
    hidden = (silu_gate * up).astype(jnp.bfloat16)
    output = jnp.dot(hidden, down_weight, preferred_element_type=jnp.float32).astype(jnp.bfloat16)
    grad_hidden = lax.dot_general(cotangent, down_weight, (((1,), (1,)), ((), ())), preferred_element_type=jnp.float32)
    grad_up_act = (grad_hidden * silu_gate).astype(jnp.bfloat16)
    grad_gate_act = (grad_hidden * up * sigma * (1.0 + gate * (1.0 - sigma))).astype(jnp.bfloat16)
    grad_down = lax.dot_general(hidden, cotangent, (((0,), (0,)), ((), ())), preferred_element_type=jnp.float32).astype(jnp.bfloat16)
    grad_gate = lax.dot_general(tokens, grad_gate_act, (((0,), (0,)), ((), ())), preferred_element_type=jnp.float32).astype(jnp.bfloat16)
    grad_up = lax.dot_general(tokens, grad_up_act, (((0,), (0,)), ((), ())), preferred_element_type=jnp.float32).astype(jnp.bfloat16)
    back_gate = lax.dot_general(grad_gate_act, gate_weight, (((1,), (1,)), ((), ())), preferred_element_type=jnp.float32)
    back_up = lax.dot_general(grad_up_act, up_weight, (((1,), (1,)), ((), ())), preferred_element_type=jnp.float32)
    grad_tokens = (back_gate + back_up).astype(jnp.bfloat16)
    return output, grad_tokens, grad_gate, grad_up, grad_down
```

```python
import jax
import jax.numpy as jnp
from jax import lax
from jax.experimental import pallas as pl
from jax.experimental.pallas import tpu as pltpu
from jax.sharding import PartitionSpec as P

MESH = pl.DeviceIdType.MESH
F32 = jnp.float32
BF16 = jnp.bfloat16

ORDER = (4, 3, 5, 2, 6, 1, 7, 0)
PIECE = 16
BLOCK = 256
HALF = 128
RIGHTWARD = (7, 6, 4, 2, 0)
LEFTWARD = (7, 5, 3, 1, 0)


def dot(a, b, ca, cb):
    return lax.dot_general(a, b, (((ca,), (cb,)), ((), ())), preferred_element_type=F32)


def kernel(
    tok, gw, uw, dw, cot,
    out, gt, gg, gu, gd,
    X, W, WD, WT, sent, got, part, final, H,
    S, SR, T, RX, U, UB, RY, acc, accd, gsend, gdsend,
    w_s, w_r, ag_s, ag_r, fw_s, fw_r, rs_s, rs_r, ga_s, ga_r, sx_s, sx_r, xy_s, xy_r, gr_s, gr_r,
):
    row, col = lax.axis_index("row"), lax.axis_index("col")
    z, k = row // 2, row % 2
    x, y = col // 4, col % 4
    other = 1 - k
    sibling = (z * 2 + other, col)
    right = (lax.rem(z + 1, 8) * 2 + k, col)
    left = (lax.rem(z + 7, 8) * 2 + k, col)

    def xpeer(i):
        return (row, lax.rem(x + i, 4) * 4 + y)

    def ypeer(i):
        return (row, x * 4 + lax.rem(y + i, 4))

    def copy(src, dst, s, r, device):
        return pltpu.make_async_remote_copy(
            src_ref=src, dst_ref=dst, send_sem=s, recv_sem=r, device_id=device, device_id_type=MESH
        )

    started = {}

    def start(key, c):
        c.start()
        started[key] = c

    def arrive(*key):
        started[key].wait_recv()

    barrier = pltpu.get_barrier_semaphore()
    for device in [sibling, right, left] + [xpeer(i) for i in (1, 2, 3)] + [ypeer(i) for i in (1, 2, 3)]:
        pl.semaphore_signal(barrier, inc=1, device_id=device, device_id_type=MESH)

    for a, ref in enumerate((tok, cot)):
        for o, d in enumerate(ORDER):
            j = lax.rem(z + d, 8)
            X[a, k, x, y, o] = ref[pl.ds(pl.multiple_of(j * PIECE, PIECE), PIECE), :]
    pl.semaphore_wait(barrier, 9)

    def gather1(a, c):
        for cls, peer in ((0, xpeer), (1, ypeer)):
            o = 4 * c + 2 * cls
            ref = X.at[a, k, x, y, pl.ds(o, 2)]
            for i in (1, 2, 3):
                start(
                    ("gather", a, c, cls, 0, i),
                    copy(ref, ref, ag_s.at[a, c, cls, 0, i - 1], ag_r.at[a, c, cls, 0, i - 1], peer(i)),
                )

    def gather2(a, c):
        for cls, peer in ((0, ypeer), (1, xpeer)):
            o = 4 * c + 2 * cls
            for i in (1, 2, 3):
                arrive("gather", a, c, cls, 0, i)
            ref = X.at[a, k, :, y, pl.ds(o, 2)] if cls == 0 else X.at[a, k, x, :, pl.ds(o, 2)]
            for i in (1, 2, 3):
                start(
                    ("gather", a, c, cls, 1, i),
                    copy(ref, ref, ag_s.at[a, c, cls, 1, i - 1], ag_r.at[a, c, cls, 1, i - 1], peer(i)),
                )

    def gather3(a, c):
        for cls in range(2):
            for i in (1, 2, 3):
                arrive("gather", a, c, cls, 1, i)
        ref = X.at[a, k, :, :, pl.ds(4 * c, 4)]
        start(("pair", a, c), copy(ref, ref, fw_s.at[a, c], fw_r.at[a, c], sibling))

    def gather4(a, c):
        arrive("pair", a, c)

    gather1(0, 0)
    gather1(1, 0)
    gather1(0, 1)
    gather1(1, 1)

    mine = pl.ds(pl.multiple_of(k * BLOCK, BLOCK), BLOCK)
    theirs = pl.ds(pl.multiple_of(other * BLOCK, BLOCK), BLOCK)
    start(("weight", 0), copy(gw.at[:, theirs], W.at[0, k], w_s.at[0], w_r.at[0], sibling))
    start(("weight", 1), copy(uw.at[:, theirs], W.at[1, k], w_s.at[1], w_r.at[1], sibling))
    start(("weight", 2), copy(dw.at[theirs, :], WD.at[k], w_s.at[2], w_r.at[2], sibling))
    W[0, k] = gw[:, mine]
    W[1, k] = uw[:, mine]
    WD[k] = dw[mine, :]
    for dr in range(2):
        for a in range(3):
            got[a, dr, 0, pl.ds(HALF * (1 - dr), HALF), :] = jnp.zeros((HALF, BLOCK), BF16)

    gather2(0, 0)
    for i in range(3):
        arrive("weight", i)
    width = dw.shape[1]
    eye = (
        lax.broadcasted_iota(jnp.int32, (width, width), 0) == lax.broadcasted_iota(jnp.int32, (width, width), 1)
    ).astype(BF16)
    for h in range(2):
        WT[h] = dot(eye, WD[h], 1, 1).astype(BF16)
    gather3(0, 0)
    gather2(1, 0)
    gather2(0, 1)
    gather4(0, 0)

    def local(a, o, first, rows):
        total = None
        for h in range(2):
            block = X[a // 2, h, pl.ds(first, rows // 64), :, o].reshape(rows, width)
            p = dot(block, W[a, h] if a < 2 else WT[h], 1, 0)
            total = p if total is None else total + p
        return total

    def chain(a, dr, s, rows):
        return copy(
            sent.at[a, dr, s, rows],
            got.at[a, dr, s, rows],
            rs_s.at[a, dr, s],
            rs_r.at[a, dr, s],
            right if dr == 0 else left,
        )

    def half(dr):
        return pl.ds(HALF * dr, HALF)

    def step0(a):
        for dr in range(2):
            sent[a, dr, 0, half(dr), :] = local(a, 0, 2 * dr, HALF).astype(BF16)
            start(("chain", a, dr, 0), chain(a, dr, 0, half(dr)))

    def step(a, s):
        for dr in range(2):
            part[dr] = local(a, 2 * s - 1 + dr, 0, BLOCK)
        for dr in range(2):
            arrive("chain", a, dr, s - 1)
            sent[a, dr, s] = (part[dr] + got[a, dr, s - 1].astype(F32)).astype(BF16)
            start(("chain", a, dr, s), chain(a, dr, s, pl.ds(0, BLOCK)))

    def finish(a):
        final[a] = local(a, 7, 0, BLOCK)
        for dr in range(2):
            arrive("chain", a, dr, 3)
        final[a] += got[a, 0, 3].astype(F32) + got[a, 1, 3].astype(F32)

    step0(0)
    step0(1)
    gather3(1, 0)
    gather2(1, 1)
    gather3(0, 1)
    gather4(1, 0)
    step0(2)
    gather3(1, 1)
    step(0, 1)
    step(1, 1)
    step(2, 1)
    gather4(0, 1)
    step(0, 2)
    step(1, 2)
    gather4(1, 1)
    step(2, 2)
    for a in range(3):
        step(a, 3)

    def relay(m, dr, s):
        places = RIGHTWARD if dr == 0 else LEFTWARD
        rows = half(dr) if s == 3 else pl.ds(0, BLOCK)
        lo, n = (0, 1) if m == 0 else (1, 2)
        return copy(
            H.at[pl.ds(lo, n), places[s], rows],
            H.at[pl.ds(lo, n), places[s + 1], rows],
            ga_s.at[m, dr, s],
            ga_r.at[m, dr, s],
            right if dr == 0 else left,
        )

    def relay_step(m, s):
        for dr in range(2):
            if s > 0:
                arrive("relay", m, dr, s - 1)
            start(("relay", m, dr, s), relay(m, dr, s))

    def relay_end(m):
        for dr in range(2):
            arrive("relay", m, dr, 3)

    finish(0)
    finish(1)
    gate, up = final[0], final[1]
    sigma = jax.nn.sigmoid(gate)
    H[0, 7] = ((gate * sigma) * up).astype(BF16)
    relay_step(0, 0)
    finish(2)
    gate, up, gh = final[0], final[1], final[2]
    sigma = jax.nn.sigmoid(gate)
    H[1, 7] = (gh * up * sigma * (1.0 + gate * (1.0 - sigma))).astype(BF16)
    H[2, 7] = (gh * (gate * sigma)).astype(BF16)
    relay_step(1, 0)

    def products(i, c):
        def body(o, carry):
            place = 4 * c + o
            for h in range(2):
                if i == 0:
                    p = dot(H[0, place], WD[h], 1, 0)
                else:
                    p = dot(H[1, place], W[0, h], 1, 1) + dot(H[2, place], W[1, h], 1, 1)
                S[i, c, h, :, :, o] = p.reshape(4, 4, PIECE, width)
            return carry

        lax.fori_loop(0, 4, body, 0)
        start(("cores", i, c), cores(i, c))

    def cores(i, c):
        return copy(S.at[i, c, other], SR.at[i, c], sx_s.at[i, c], sx_r.at[i, c], sibling)

    def scatter(i, c, cls, phase, n):
        if phase == 0:
            if cls == 0:
                src, peer = T.at[i, c, lax.rem(x + n, 4), :, pl.ds(0, 2)], xpeer(n)
            else:
                src, peer = T.at[i, c, :, lax.rem(y + n, 4), pl.ds(2, 2)], ypeer(n)
            dst = RX.at[i, c, cls, n - 1]
        else:
            if cls == 0:
                src, peer = UB.at[i, c, 0, lax.rem(y + n, 4)], ypeer(n)
            else:
                src, peer = UB.at[i, c, 1, lax.rem(x + n, 4)], xpeer(n)
            dst = RY.at[i, c, cls, n - 1]
        return copy(src, dst, xy_s.at[i, c, cls, phase, n - 1], xy_r.at[i, c, cls, phase, n - 1], peer)

    def scatter1(i, c):
        arrive("cores", i, c)

        def body(v, carry):
            T[i, c, v] = S[i, c, k, v] + SR[i, c, v]
            return carry

        lax.fori_loop(0, 4, body, 0)
        for cls in range(2):
            for n in (1, 2, 3):
                start(("scatter", i, c, cls, 0, n), scatter(i, c, cls, 0, n))

    def scatter2(i, c):
        for cls in range(2):
            if cls == 0:
                total = S[i, c, k, x, :, 0:2] + SR[i, c, x, :, 0:2]
            else:
                total = S[i, c, k, :, y, 2:4] + SR[i, c, :, y, 2:4]
            for n in (1, 2, 3):
                arrive("scatter", i, c, cls, 0, n)
                total = total + RX[i, c, cls, n - 1]
            U[i, c, cls] = total
            UB[i, c, cls] = total
            for n in (1, 2, 3):
                start(("scatter", i, c, cls, 1, n), scatter(i, c, cls, 1, n))

    def scatter3(i, c):
        ref = (out, gt)[i]
        for cls in range(2):
            total = U[i, c, cls, y if cls == 0 else x]
            for n in (1, 2, 3):
                arrive("scatter", i, c, cls, 1, n)
                total = total + RY[i, c, cls, n - 1]
            for p in range(2):
                j = lax.rem(z + ORDER[4 * c + 2 * cls + p], 8)
                ref[pl.ds(pl.multiple_of(j * PIECE, PIECE), PIECE), :] = total[p].astype(BF16)

    def grad(n):
        def body(o, carry):
            for h in range(2):
                if n == 2:
                    p = dot(H[0, o], X[1, h, :, :, o].reshape(BLOCK, width), 0, 0)
                    accd[h] = jnp.where(o == 0, p, accd[h] + p)
                else:
                    p = dot(X[0, h, :, :, o].reshape(BLOCK, width), H[1 + n, o], 0, 0)
                    acc[n, h] = jnp.where(o == 0, p, acc[n, h] + p)
            return carry

        lax.fori_loop(0, 8, body, 0)
        if n == 2:
            gdsend[...] = accd[other].astype(BF16)
            gd[mine, :] = accd[k].astype(BF16)
        else:
            gsend[n] = acc[n, other].astype(BF16)
            (gg, gu)[n][:, mine] = acc[n, k].astype(BF16)
        start(("grad", n), grad_copy(n))

    def grad_copy(n):
        if n == 2:
            return copy(gdsend, gd.at[mine, :], gr_s.at[2], gr_r.at[2], sibling)
        return copy(gsend.at[n], (gg, gu)[n].at[:, mine], gr_s.at[n], gr_r.at[n], sibling)

    relay_step(0, 1)
    relay_step(1, 1)
    relay_step(0, 2)
    products(0, 1)
    relay_step(1, 2)
    products(1, 1)
    scatter1(0, 1)
    relay_step(0, 3)
    scatter1(1, 1)
    scatter2(0, 1)
    relay_step(1, 3)
    scatter2(1, 1)
    relay_end(0)
    products(0, 0)
    grad(2)
    scatter1(0, 0)
    relay_end(1)
    products(1, 0)
    scatter2(0, 0)
    scatter1(1, 0)
    grad(0)
    scatter2(1, 0)
    grad(1)
    scatter3(0, 1)
    scatter3(1, 1)
    scatter3(0, 0)
    scatter3(1, 0)
    for n in (2, 0, 1):
        arrive("grad", n)
    for c in started.values():
        c.wait_send()


def body(tokens, gate_weight, up_weight, down_weight, cotangent):
    n_tok, width = tokens.shape
    hidden = gate_weight.shape[1]
    vmem = pl.BlockSpec(memory_space=pltpu.VMEM)
    dma = pltpu.SemaphoreType.DMA
    V = pltpu.VMEM
    scratch = [
        V((2, 2, 4, 4, 8, PIECE, width), BF16),
        V((2, 2, width, BLOCK), BF16),
        V((2, BLOCK, width), BF16),
        V((2, width, BLOCK), BF16),
        V((3, 2, 4, BLOCK, BLOCK), BF16),
        V((3, 2, 4, BLOCK, BLOCK), BF16),
        V((2, BLOCK, BLOCK), F32),
        V((3, BLOCK, BLOCK), F32),
        V((3, 8, BLOCK, BLOCK), BF16),
        V((2, 2, 2, 4, 4, 4, PIECE, width), F32),
        V((2, 2, 4, 4, 4, PIECE, width), F32),
        V((2, 2, 4, 4, 4, PIECE, width), F32),
        V((2, 2, 2, 3, 4, 2, PIECE, width), F32),
        V((2, 2, 2, 4, 2, PIECE, width), F32),
        V((2, 2, 2, 4, 2, PIECE, width), F32),
        V((2, 2, 2, 3, 2, PIECE, width), F32),
        V((2, 2, width, BLOCK), F32),
        V((2, BLOCK, width), F32),
        V((2, width, BLOCK), BF16),
        V((BLOCK, width), BF16),
        dma((3,)), dma((3,)),
        dma((2, 2, 2, 2, 3)), dma((2, 2, 2, 2, 3)),
        dma((2, 2)), dma((2, 2)),
        dma((3, 2, 4)), dma((3, 2, 4)),
        dma((2, 2, 4)), dma((2, 2, 4)),
        dma((2, 2)), dma((2, 2)),
        dma((2, 2, 2, 2, 3)), dma((2, 2, 2, 2, 3)),
        dma((3,)), dma((3,)),
    ]
    return pl.pallas_call(
        kernel,
        out_shape=(
            jax.ShapeDtypeStruct((n_tok, width), BF16),
            jax.ShapeDtypeStruct((n_tok, width), BF16),
            jax.ShapeDtypeStruct((width, hidden), BF16),
            jax.ShapeDtypeStruct((width, hidden), BF16),
            jax.ShapeDtypeStruct((hidden, width), BF16),
        ),
        in_specs=[vmem] * 5,
        out_specs=(vmem,) * 5,
        scratch_shapes=scratch,
        name="feed_forward",
        compiler_params=pltpu.CompilerParams(
            collective_id=0, has_side_effects=True, vmem_limit_bytes=56 * 2**20
        ),
    )(tokens, gate_weight, up_weight, down_weight, cotangent)


def solution(mesh):
    return jax.shard_map(
        body,
        mesh=mesh,
        in_specs=(
            P("col", "row"),
            P("row", "col"),
            P("row", "col"),
            P("col", "row"),
            P("col", "row"),
        ),
        out_specs=(
            P("col", "row"),
            P("col", "row"),
            P("row", "col"),
            P("row", "col"),
            P("col", "row"),
        ),
        check_vma=False,
    )
```

```python
import jax
import jax.numpy as jnp
from jax import lax
from jax.experimental import pallas as pl
from jax.experimental.pallas import tpu as pltpu
from jax.sharding import PartitionSpec as P

MESH = pl.DeviceIdType.MESH
F32 = jnp.float32
BF16 = jnp.bfloat16

ORDER = (4, 3, 5, 0, 2, 1, 6, 7)
PLACE = {d: o for o, d in enumerate(ORDER)}
PIECE = 16
BLOCK = 256
HALF = 128
RIGHTWARD = tuple(PLACE[d] for d in (0, 7, 6, 5, 4))
LEFTWARD = tuple(PLACE[d] for d in (0, 1, 2, 3, 4))
NEAR = ((0, 4, 2, 0, 16), (1, 6, 2, 0, 16))
FAR = ((0, 0, 2, 0, 16), (1, 2, 2, 0, 16))
MIDDLE = ((0, 1, 1, 0, 16), (1, 2, 2, 0, 16))
LAST = ((0, 0, 1, 0, 8), (1, 0, 1, 8, 8))
PARTS = {(0, 0): NEAR, (0, 1): FAR, (1, 0): NEAR, (1, 1): MIDDLE, (1, 2): LAST}


def dot(a, b, ca, cb):
    return lax.dot_general(a, b, (((ca,), (cb,)), ((), ())), preferred_element_type=F32)


def identity(n):
    rows = lax.broadcasted_iota(jnp.int32, (n, n), 0)
    return (rows == lax.broadcasted_iota(jnp.int32, (n, n), 1)).astype(BF16)


def kernel(
    tok, gw, uw, dw, cot,
    out, gt, gg, gu, gd,
    acts, weights, rows_in, X, W, sent, got, part, final, H,
    S, SR, T, RX, U, RY, acc, gsend, ggot, grads, rows_out, results,
    in_s, out_s, w_s, w_r, ag_s, ag_r, fw_s, fw_r, rs_s, rs_r, ga_s, ga_r, sx_s, sx_r, xy_s, xy_r, gr_s, gr_r,
):
    row, col = lax.axis_index("row"), lax.axis_index("col")
    z, k = row // 2, row % 2
    x, y = col // 4, col % 4
    other = 1 - k
    width = gw.shape[0]
    sibling = (z * 2 + other, col)
    right = (lax.rem(z + 1, 8) * 2 + k, col)
    left = (lax.rem(z + 7, 8) * 2 + k, col)
    xpeers = {i: (row, lax.rem(x + i, 4) * 4 + y) for i in (1, 2, 3)}
    ypeers = {i: (row, x * 4 + lax.rem(y + i, 4)) for i in (1, 2, 3)}
    peers = (xpeers, ypeers)

    def copy(src, dst, s, r, device):
        return pltpu.make_async_remote_copy(
            src_ref=src, dst_ref=dst, send_sem=s, recv_sem=r, device_id=device, device_id_type=MESH
        )

    started = {}

    def start(key, c):
        c.start()
        started[key] = c

    def arrive(*key):
        started[key].wait_recv()

    barrier = pltpu.get_barrier_semaphore()
    for device in [sibling, right, left, *xpeers.values(), *ypeers.values()]:
        pl.semaphore_signal(barrier, inc=1, device_id=device, device_id_type=MESH)

    loads = [
        pltpu.make_async_copy(src, dst, in_s.at[i])
        for i, (src, dst) in enumerate(
            ((tok, acts.at[0]), (cot, acts.at[1]), (gw, weights.at[0]), (uw, weights.at[1]), (dw, weights.at[2]))
        )
    ]
    for c in loads:
        c.start()

    def pieces(a):
        loads[a].wait()
        rows_in[a] = dot(identity(HALF), acts[a], 1, 1).astype(BF16)
        for o, d in enumerate(ORDER):
            j = lax.rem(z + d, 8)
            X[a, k, x, y, o] = rows_in[a, pl.ds(pl.multiple_of(j * PIECE, PIECE), PIECE), :]

    def gather1(a, c):
        for cls in range(2):
            ref = X.at[a, k, x, y, pl.ds(4 * c + 2 * cls, 2)]
            for i in (1, 2, 3):
                start(
                    ("gather", a, c, cls, 0, i),
                    copy(ref, ref, ag_s.at[a, c, cls, 0, i - 1], ag_r.at[a, c, cls, 0, i - 1], peers[cls][i]),
                )

    def gather2(a, c):
        for cls in range(2):
            places = pl.ds(4 * c + 2 * cls, 2)
            for i in (1, 2, 3):
                arrive("gather", a, c, cls, 0, i)
            ref = X.at[a, k, :, y, places] if cls == 0 else X.at[a, k, x, :, places]
            for i in (1, 2, 3):
                start(
                    ("gather", a, c, cls, 1, i),
                    copy(ref, ref, ag_s.at[a, c, cls, 1, i - 1], ag_r.at[a, c, cls, 1, i - 1], peers[1 - cls][i]),
                )

    def gather3(a, c):
        for cls in range(2):
            for i in (1, 2, 3):
                arrive("gather", a, c, cls, 1, i)
        ref = X.at[a, k, :, :, pl.ds(4 * c, 4)]
        start(("pair", a, c), copy(ref, ref, fw_s.at[a, c], fw_r.at[a, c], sibling))

    def gather4(a, c):
        arrive("pair", a, c)

    mine = pl.ds(pl.multiple_of(k * BLOCK, BLOCK), BLOCK)
    theirs = pl.ds(pl.multiple_of(other * BLOCK, BLOCK), BLOCK)

    def swap_weights():
        for i in range(3):
            loads[2 + i].wait()
            start(("weight", i), copy(weights.at[i, :, theirs], W.at[i, k], w_s.at[i], w_r.at[i], sibling))
        for i in range(3):
            W[i, k] = weights[i, :, mine]

    def local(a, o, first, rows):
        total = None
        for h in range(2):
            block = X[a // 2, h, pl.ds(first, rows // 64), :, o].reshape(rows, width)
            p = dot(block, W[a, h], 1, 0)
            total = p if total is None else total + p
        return total

    def half(dr):
        return pl.ds(HALF * dr, HALF)

    def chain(a, dr, s, rows):
        start(
            ("chain", a, dr, s),
            copy(
                sent.at[a, dr, s, rows],
                got.at[a, dr, s, rows],
                rs_s.at[a, dr, s],
                rs_r.at[a, dr, s],
                (right, left)[dr],
            ),
        )

    def step0(a):
        for dr in range(2):
            sent[a, dr, 0, half(dr), :] = local(a, PLACE[4], 2 * dr, HALF).astype(BF16)
            chain(a, dr, 0, half(dr))

    def step(a, s):
        for dr in range(2):
            part[dr] = local(a, PLACE[(4 - s, 4 + s)[dr]], 0, BLOCK)
        for dr in range(2):
            arrive("chain", a, dr, s - 1)
            if s == 1:
                sent[a, dr, s, half(dr), :] = (part[dr, half(dr), :] + got[a, dr, 0, half(dr), :].astype(F32)).astype(BF16)
                sent[a, dr, s, half(1 - dr), :] = part[dr, half(1 - dr), :].astype(BF16)
            else:
                sent[a, dr, s] = (part[dr] + got[a, dr, s - 1].astype(F32)).astype(BF16)
            chain(a, dr, s, pl.ds(0, BLOCK))

    def finish(a):
        final[a] = local(a, PLACE[0], 0, BLOCK)
        for dr in range(2):
            arrive("chain", a, dr, 3)
        final[a] += got[a, 0, 3].astype(F32) + got[a, 1, 3].astype(F32)

    def relay_step(m, s):
        lo, n = (0, 1) if m == 0 else (1, 2)
        for dr in range(2):
            places = (RIGHTWARD, LEFTWARD)[dr]
            rows = half(dr) if s == 3 else pl.ds(0, BLOCK)
            if s > 0:
                arrive("relay", m, dr, s - 1)
            start(
                ("relay", m, dr, s),
                copy(
                    H.at[pl.ds(lo, n), places[s], rows],
                    H.at[pl.ds(lo, n), places[s + 1], rows],
                    ga_s.at[m, dr, s],
                    ga_r.at[m, dr, s],
                    (right, left)[dr],
                ),
            )

    def relay_end(m):
        for dr in range(2):
            arrive("relay", m, dr, 3)

    def activate():
        gate, up = final[0], final[1]
        H[0, PLACE[0]] = ((gate * jax.nn.sigmoid(gate)) * up).astype(BF16)

    def activate_back():
        gate, up, gh = final[0], final[1], final[2]
        sigma = jax.nn.sigmoid(gate)
        H[1, PLACE[0]] = (gh * up * sigma * (1.0 + gate * (1.0 - sigma))).astype(BF16)
        H[2, PLACE[0]] = (gh * (gate * sigma)).astype(BF16)

    def products(i, g, lo, n):
        def body(o, carry):
            for h in range(2):
                if i == 0:
                    p = dot(H[0, o], W[2, h], 1, 1)
                else:
                    p = dot(H[1, o], W[0, h], 1, 1) + dot(H[2, o], W[1, h], 1, 1)
                S[i, h, :, :, o] = p.reshape(4, 4, PIECE, width)
            return carry

        if n == 1:
            body(lo, 0)
        else:
            lax.fori_loop(lo, lo + n, body, 0)
        span = pl.ds(lo, n)
        start(
            ("cores", i, g),
            copy(S.at[i, other, :, :, span], SR.at[i, :, :, span], sx_s.at[i, g], sx_r.at[i, g], sibling),
        )

    def scatter1(i, g):
        arrive("cores", i, g)
        for cls, lo, n, r, m in PARTS[i, g]:
            span, rows = pl.ds(lo, n), pl.ds(r, m)
            T[i, :, :, span, rows] = S[i, k, :, :, span, rows] + SR[i, :, :, span, rows]
            for q in (1, 2, 3):
                if cls == 0:
                    src = T.at[i, lax.rem(x + q, 4), :, span, rows]
                else:
                    src = T.at[i, :, lax.rem(y + q, 4), span, rows]
                start(
                    ("scatter", i, g, cls, 0, q),
                    copy(
                        src,
                        RX.at[i, q - 1, :, span, rows],
                        xy_s.at[i, g, cls, 0, q - 1],
                        xy_r.at[i, g, cls, 0, q - 1],
                        peers[cls][q],
                    ),
                )

    def scatter2(i, g):
        for cls, lo, n, r, m in PARTS[i, g]:
            span, rows = pl.ds(lo, n), pl.ds(r, m)
            total = T[i, x, :, span, rows] if cls == 0 else T[i, :, y, span, rows]
            for q in (1, 2, 3):
                arrive("scatter", i, g, cls, 0, q)
                total = total + RX[i, q - 1, :, span, rows]
            U[i, :, span, rows] = total
            for q in (1, 2, 3):
                at = lax.rem(y + q, 4) if cls == 0 else lax.rem(x + q, 4)
                start(
                    ("scatter", i, g, cls, 1, q),
                    copy(
                        U.at[i, at, span, rows],
                        RY.at[i, q - 1, span, rows],
                        xy_s.at[i, g, cls, 1, q - 1],
                        xy_r.at[i, g, cls, 1, q - 1],
                        peers[1 - cls][q],
                    ),
                )

    def scatter3(i, g):
        for cls, lo, n, r, m in PARTS[i, g]:
            span, rows = pl.ds(lo, n), pl.ds(r, m)
            total = U[i, y if cls == 0 else x, span, rows]
            for q in (1, 2, 3):
                arrive("scatter", i, g, cls, 1, q)
                total = total + RY[i, q - 1, span, rows]
            for p in range(n):
                j = lax.rem(z + ORDER[lo + p], 8)
                rows_out[i, pl.ds(pl.multiple_of(j * PIECE + r, 8), m), :] = total[p]

    stores = []

    def store(src, dst):
        c = pltpu.make_async_copy(src, dst, out_s.at[len(stores)])
        c.start()
        stores.append(c)

    def deliver(i):
        results[i] = dot(identity(width), rows_out[i].astype(BF16), 1, 1).astype(BF16)
        store(results.at[i], (out, gt)[i])

    def grad(n, lo, hi):
        a, b = ((0, 1), (0, 2), (1, 0))[n]

        def body(o, carry):
            for h in range(2):
                acc[n, h] += dot(X[a, h, :, :, o].reshape(BLOCK, width), H[b, o], 0, 0)
            return carry

        if hi - lo == 1:
            body(lo, 0)
        else:
            lax.fori_loop(lo, hi, body, 0)

    def grad_swap(n):
        gsend[n] = acc[n, other].astype(BF16)
        start(("grad", n), copy(gsend.at[n], ggot.at[n], gr_s.at[n], gr_r.at[n], sibling))
        grads[n, :, mine] = acc[n, k].astype(BF16)

    def grad_end(n):
        arrive("grad", n)
        grads[n, :, theirs] = ggot[n]
        store(grads.at[n], (gg, gu, gd)[n])

    pieces(0)
    pl.semaphore_wait(barrier, 9)
    gather1(0, 0)
    swap_weights()
    gather1(0, 1)
    pieces(1)
    gather2(0, 0)
    gather1(1, 0)
    acc[...] = jnp.zeros_like(acc)
    gather2(0, 1)
    gather3(0, 0)
    gather2(1, 0)
    gather1(1, 1)
    for i in range(3):
        arrive("weight", i)
    gather4(0, 0)
    step0(0)
    step0(1)
    gather3(0, 1)
    step(0, 1)
    step(1, 1)
    gather3(1, 0)
    gather2(1, 1)
    gather4(0, 1)
    step(0, 2)
    step(1, 2)
    gather4(1, 0)
    step0(2)
    gather3(1, 1)
    step(0, 3)
    step(1, 3)
    step(2, 1)
    gather4(1, 1)
    finish(0)
    finish(1)
    activate()
    relay_step(0, 0)
    step(2, 2)
    step(2, 3)
    relay_step(0, 1)
    finish(2)
    activate_back()
    relay_step(1, 0)
    relay_step(0, 2)
    products(0, 0, 4, 4)
    relay_step(1, 1)
    scatter1(0, 0)
    relay_step(0, 3)
    grad(2, 4, 8)
    relay_step(1, 2)
    products(1, 0, 4, 4)
    relay_end(0)
    products(0, 1, 0, 4)
    scatter1(1, 0)
    grad(2, 0, 4)
    relay_step(1, 3)
    products(1, 1, 1, 3)
    scatter2(0, 0)
    scatter1(0, 1)
    scatter2(1, 0)
    grad_swap(2)
    scatter1(1, 1)
    grad(0, 1, 8)
    grad(1, 1, 8)
    relay_end(1)
    products(1, 2, 0, 1)
    scatter2(0, 1)
    grad(0, 0, 1)
    grad_swap(0)
    scatter1(1, 2)
    scatter2(1, 1)
    grad(1, 0, 1)
    grad_swap(1)
    scatter3(0, 0)
    scatter3(0, 1)
    deliver(0)
    grad_end(2)
    scatter2(1, 2)
    scatter3(1, 0)
    grad_end(0)
    grad_end(1)
    scatter3(1, 1)
    scatter3(1, 2)
    deliver(1)
    for c in stores:
        c.wait()
    for c in started.values():
        c.wait_send()


def hand_over(*refs):
    sems = refs[10]
    copies = [pltpu.make_async_copy(refs[i], refs[5 + i], sems.at[i]) for i in range(5)]
    for c in copies:
        c.start()
    for c in copies:
        c.wait()


def body(tokens, gate_weight, up_weight, down_weight, cotangent):
    n_tok, width = tokens.shape
    hidden = gate_weight.shape[1]
    dma = pltpu.SemaphoreType.DMA
    V = pltpu.VMEM
    act = jax.ShapeDtypeStruct((width, n_tok), BF16)
    weight = jax.ShapeDtypeStruct((width, hidden), BF16)
    shapes = (act, act, weight, weight, weight)
    scratch = [
        V((2, width, n_tok), BF16),
        V((3, width, hidden), BF16),
        V((2, n_tok, width), BF16),
        V((2, 2, 4, 4, 8, PIECE, width), BF16),
        V((3, 2, width, BLOCK), BF16),
        V((3, 2, 4, BLOCK, BLOCK), BF16),
        V((3, 2, 4, BLOCK, BLOCK), BF16),
        V((2, BLOCK, BLOCK), F32),
        V((3, BLOCK, BLOCK), F32),
        V((3, 8, BLOCK, BLOCK), BF16),
        V((2, 2, 4, 4, 8, PIECE, width), F32),
        V((2, 4, 4, 8, PIECE, width), F32),
        V((2, 4, 4, 8, PIECE, width), F32),
        V((2, 3, 4, 8, PIECE, width), F32),
        V((2, 4, 8, PIECE, width), F32),
        V((2, 3, 8, PIECE, width), F32),
        V((3, 2, width, BLOCK), F32),
        V((3, width, BLOCK), BF16),
        V((3, width, BLOCK), BF16),
        V((3, width, hidden), BF16),
        V((2, n_tok, width), F32),
        V((2, width, n_tok), BF16),
        dma((5,)), dma((5,)),
        dma((3,)), dma((3,)),
        dma((2, 2, 2, 2, 3)), dma((2, 2, 2, 2, 3)),
        dma((2, 2)), dma((2, 2)),
        dma((3, 2, 4)), dma((3, 2, 4)),
        dma((2, 2, 4)), dma((2, 2, 4)),
        dma((2, 3)), dma((2, 3)),
        dma((2, 3, 2, 2, 3)), dma((2, 3, 2, 2, 3)),
        dma((3,)), dma((3,)),
    ]
    anywhere = pl.BlockSpec(memory_space=pl.ANY)
    held = pl.pallas_call(
        kernel,
        out_shape=shapes,
        in_specs=[anywhere] * 5,
        out_specs=(anywhere,) * 5,
        scratch_shapes=scratch,
        name="feed_forward",
        compiler_params=pltpu.CompilerParams(
            collective_id=0, has_side_effects=True, vmem_limit_bytes=56 * 2**20
        ),
    )(tokens.T, gate_weight, up_weight, down_weight.T, cotangent.T)
    results = pl.pallas_call(
        hand_over,
        out_shape=shapes,
        in_specs=[anywhere] * 5,
        out_specs=(anywhere,) * 5,
        scratch_shapes=[dma((5,))],
        name="hand_over",
        compiler_params=pltpu.CompilerParams(vmem_limit_bytes=60 * 2**20),
    )(*held)
    return results[0].T, results[1].T, results[2], results[3], results[4].T


def solution(mesh):
    return jax.shard_map(
        body,
        mesh=mesh,
        in_specs=(
            P("col", "row"),
            P("row", "col"),
            P("row", "col"),
            P("col", "row"),
            P("col", "row"),
        ),
        out_specs=(
            P("col", "row"),
            P("col", "row"),
            P("row", "col"),
            P("row", "col"),
            P("col", "row"),
        ),
        check_vma=False,
    )
```

```python
import jax
import jax.numpy as jnp
from jax import lax
from jax.experimental import pallas as pl
from jax.experimental.pallas import tpu as pltpu
from jax.sharding import PartitionSpec as P

MESH = pl.DeviceIdType.MESH
F32 = jnp.float32
BF16 = jnp.bfloat16

ORDER = (4, 3, 5, 0, 2, 1, 6, 7)
PLACE = {d: o for o, d in enumerate(ORDER)}
PIECE = 16
LANES = 128
TAIL = 64
BLOCK = 256
HALF = 128
RIGHTWARD = tuple(PLACE[d] for d in (0, 7, 6, 5, 4))
LEFTWARD = tuple(PLACE[d] for d in (0, 1, 2, 3, 4))
NEAR = ((0, 4, 2, 0, 24), (1, 6, 2, 0, 24))
FAR = ((0, 0, 2, 0, 24), (1, 2, 2, 0, 24))
MIDDLE = ((0, 1, 1, 0, 24), (1, 2, 2, 0, 24))
LAST = ((0, 0, 1, 0, 16), (1, 0, 1, 16, 8))
PARTS = {(0, 0): NEAR, (0, 1): FAR, (1, 0): NEAR, (1, 1): MIDDLE, (1, 2): LAST}


def dot(a, b, ca, cb):
    return lax.dot_general(a, b, (((ca,), (cb,)), ((), ())), preferred_element_type=F32)


def identity(n):
    rows = lax.broadcasted_iota(jnp.int32, (n, n), 0)
    return (rows == lax.broadcasted_iota(jnp.int32, (n, n), 1)).astype(BF16)


def kernel(
    tok, gw, uw, dw, cot,
    out, gt, gg, gu, gd,
    acts, weights, rows_in, X, W, WE, WP, sent, got, part, final, H,
    S, SR, T, RX, U, RY, acc, gsend, ggot, grads, rows_out, results,
    in_s, out_s, w_s, w_r, ag_s, ag_r, fw_s, fw_r, rs_s, rs_r, ga_s, ga_r, sx_s, sx_r, xy_s, xy_r, gr_s, gr_r,
):
    row, col = lax.axis_index("row"), lax.axis_index("col")
    z, k = row // 2, row % 2
    x, y = col // 4, col % 4
    other = 1 - k
    width = gw.shape[0]
    sibling = (z * 2 + other, col)
    right = (lax.rem(z + 1, 8) * 2 + k, col)
    left = (lax.rem(z + 7, 8) * 2 + k, col)
    xpeers = {i: (row, lax.rem(x + i, 4) * 4 + y) for i in (1, 2, 3)}
    ypeers = {i: (row, x * 4 + lax.rem(y + i, 4)) for i in (1, 2, 3)}
    peers = (xpeers, ypeers)

    def copy(src, dst, s, r, device):
        return pltpu.make_async_remote_copy(
            src_ref=src, dst_ref=dst, send_sem=s, recv_sem=r, device_id=device, device_id_type=MESH
        )

    started = {}

    def start(key, c):
        c.start()
        started[key] = c

    def arrive(*key):
        started[key].wait_recv()

    barrier = pltpu.get_barrier_semaphore()
    for device in [sibling, right, left, *xpeers.values(), *ypeers.values()]:
        pl.semaphore_signal(barrier, inc=1, device_id=device, device_id_type=MESH)

    first_half = lax.broadcasted_iota(jnp.int32, (PIECE, LANES), 1) < TAIL
    loads = [
        pltpu.make_async_copy(src, dst, in_s.at[i])
        for i, (src, dst) in enumerate(
            ((tok, acts.at[0]), (cot, acts.at[1]), (gw, weights.at[0]), (uw, weights.at[1]), (dw, weights.at[2]))
        )
    ]
    for c in loads:
        c.start()

    def pieces(a):
        loads[a].wait()
        one = identity(HALF)
        tails = acts[a, pl.ds(LANES, TAIL), :]
        rows_in[a, 0] = dot(one, acts[a, pl.ds(0, LANES), :], 1, 1)
        rows_in[a, 1] = dot(one, jnp.concatenate([tails, tails], axis=0), 1, 1)
        for q in range(4):
            at = [pl.ds(pl.multiple_of(lax.rem(z + ORDER[2 * q + e], 8) * PIECE, PIECE), PIECE) for e in range(2)]
            for e in range(2):
                X[a, k, x, y, q, pl.ds(e * PIECE, PIECE), :] = rows_in[a, 0, at[e], :].astype(BF16)
            X[a, k, x, y, q, pl.ds(2 * PIECE, PIECE), :] = jnp.where(
                first_half, rows_in[a, 1, at[0], :], rows_in[a, 1, at[1], :]
            ).astype(BF16)

    def gather1(a, c):
        for cls in range(2):
            ref = X.at[a, k, x, y, 2 * c + cls]
            for i in (1, 2, 3):
                start(
                    ("gather", a, c, cls, 0, i),
                    copy(ref, ref, ag_s.at[a, c, cls, 0, i - 1], ag_r.at[a, c, cls, 0, i - 1], peers[cls][i]),
                )

    def gather2(a, c):
        for cls in range(2):
            q = 2 * c + cls
            for i in (1, 2, 3):
                arrive("gather", a, c, cls, 0, i)
            ref = X.at[a, k, :, y, q] if cls == 0 else X.at[a, k, x, :, q]
            for i in (1, 2, 3):
                start(
                    ("gather", a, c, cls, 1, i),
                    copy(ref, ref, ag_s.at[a, c, cls, 1, i - 1], ag_r.at[a, c, cls, 1, i - 1], peers[1 - cls][i]),
                )

    def gather3(a, c):
        for cls in range(2):
            for i in (1, 2, 3):
                arrive("gather", a, c, cls, 1, i)
        ref = X.at[a, k, :, :, pl.ds(2 * c, 2)]
        start(("pair", a, c), copy(ref, ref, fw_s.at[a, c], fw_r.at[a, c], sibling))

    def gather4(a, c):
        arrive("pair", a, c)

    mine = pl.ds(pl.multiple_of(k * BLOCK, BLOCK), BLOCK)
    theirs = pl.ds(pl.multiple_of(other * BLOCK, BLOCK), BLOCK)

    def swap_weights():
        for i in range(3):
            loads[2 + i].wait()
            start(("weight", i), copy(weights.at[i, :, theirs], W.at[i, k], w_s.at[i], w_r.at[i], sibling))
        for i in range(3):
            W[i, k] = weights[i, :, mine]
            expand(i, k)

    def expand(i, h):
        main, tail = W[i, h, pl.ds(0, LANES), :], W[i, h, pl.ds(LANES, TAIL), :]
        none = jnp.zeros_like(tail)
        for e in range(2):
            WE[e, i, h, pl.ds(0, LANES), :] = main
            WE[e, i, h, pl.ds(LANES + e * TAIL, TAIL), :] = tail
            WE[e, i, h, pl.ds(LANES + (1 - e) * TAIL, TAIL), :] = none
        WP[i, h, pl.ds(0, LANES), :] = main
        for e in range(2):
            WP[i, h, pl.ds(LANES + e * TAIL, TAIL), :] = tail

    def expand_theirs():
        for i in range(3):
            arrive("weight", i)
            expand(i, other)

    def packed(a, h, q, e, first, rows):
        span = pl.ds(first, rows // 64)
        main = X[a, h, span, :, q, pl.ds(e * PIECE, PIECE), :].reshape(rows, LANES)
        tail = X[a, h, span, :, q, pl.ds(2 * PIECE, PIECE), :].reshape(rows, LANES)
        return jnp.concatenate([main, tail], axis=1)

    def local(a, o, first, rows):
        total = None
        for h in range(2):
            p = dot(packed(a // 2, h, o // 2, o % 2, first, rows), WE[o % 2, a, h], 1, 0)
            total = p if total is None else total + p
        return total

    def half(dr):
        return pl.ds(HALF * dr, HALF)

    def chain(a, dr, s, rows):
        start(
            ("chain", a, dr, s),
            copy(
                sent.at[a, dr, s, rows],
                got.at[a, dr, s, rows],
                rs_s.at[a, dr, s],
                rs_r.at[a, dr, s],
                (right, left)[dr],
            ),
        )

    def step0(a):
        for dr in range(2):
            sent[a, dr, 0, half(dr), :] = local(a, PLACE[4], 2 * dr, HALF).astype(BF16)
            chain(a, dr, 0, half(dr))

    def step(a, s):
        for dr in range(2):
            part[dr] = local(a, PLACE[(4 - s, 4 + s)[dr]], 0, BLOCK)
        for dr in range(2):
            arrive("chain", a, dr, s - 1)
            if s == 1:
                sent[a, dr, s, half(dr), :] = (part[dr, half(dr), :] + got[a, dr, 0, half(dr), :].astype(F32)).astype(BF16)
                sent[a, dr, s, half(1 - dr), :] = part[dr, half(1 - dr), :].astype(BF16)
            else:
                sent[a, dr, s] = (part[dr] + got[a, dr, s - 1].astype(F32)).astype(BF16)
            chain(a, dr, s, pl.ds(0, BLOCK))

    def finish(a):
        final[a] = local(a, PLACE[0], 0, BLOCK)
        for dr in range(2):
            arrive("chain", a, dr, 3)
        final[a] += got[a, 0, 3].astype(F32) + got[a, 1, 3].astype(F32)

    def relay_step(m, s):
        lo, n = (0, 1) if m == 0 else (1, 2)
        for dr in range(2):
            places = (RIGHTWARD, LEFTWARD)[dr]
            rows = half(dr) if s == 3 else pl.ds(0, BLOCK)
            if s > 0:
                arrive("relay", m, dr, s - 1)
            start(
                ("relay", m, dr, s),
                copy(
                    H.at[pl.ds(lo, n), places[s], rows],
                    H.at[pl.ds(lo, n), places[s + 1], rows],
                    ga_s.at[m, dr, s],
                    ga_r.at[m, dr, s],
                    (right, left)[dr],
                ),
            )

    def relay_end(m):
        for dr in range(2):
            arrive("relay", m, dr, 3)

    def activate():
        gate, up = final[0], final[1]
        H[0, PLACE[0]] = ((gate * jax.nn.sigmoid(gate)) * up).astype(BF16)

    def activate_back():
        gate, up, gh = final[0], final[1], final[2]
        sigma = jax.nn.sigmoid(gate)
        H[1, PLACE[0]] = (gh * up * sigma * (1.0 + gate * (1.0 - sigma))).astype(BF16)
        H[2, PLACE[0]] = (gh * (gate * sigma)).astype(BF16)

    def products(i, g, lo, n):
        def body(o, carry):
            for h in range(2):
                if i == 0:
                    p = dot(H[0, o], WP[2, h], 1, 1)
                else:
                    p = dot(H[1, o], WP[0, h], 1, 1) + dot(H[2, o], WP[1, h], 1, 1)
                S[i, h, :, :, o, pl.ds(0, PIECE), :] = p[:, :LANES].reshape(4, 4, PIECE, LANES)
                tail = p[:, LANES:].reshape(4, 4, PIECE, LANES)
                low = lax.broadcasted_iota(jnp.int32, (4, 4, 8, LANES), 3) < TAIL
                S[i, h, :, :, o, pl.ds(PIECE, 8), :] = jnp.where(low, tail[:, :, :8], tail[:, :, 8:])
            return carry

        if n == 1:
            body(lo, 0)
        else:
            lax.fori_loop(lo, lo + n, body, 0)
        span = pl.ds(lo, n)
        start(
            ("cores", i, g),
            copy(S.at[i, other, :, :, span], SR.at[i, :, :, span], sx_s.at[i, g], sx_r.at[i, g], sibling),
        )

    def scatter1(i, g):
        arrive("cores", i, g)
        for cls, lo, n, r, m in PARTS[i, g]:
            span, rows = pl.ds(lo, n), pl.ds(r, m)
            T[i, :, :, span, rows] = S[i, k, :, :, span, rows] + SR[i, :, :, span, rows]
            for q in (1, 2, 3):
                if cls == 0:
                    src = T.at[i, lax.rem(x + q, 4), :, span, rows]
                else:
                    src = T.at[i, :, lax.rem(y + q, 4), span, rows]
                start(
                    ("scatter", i, g, cls, 0, q),
                    copy(
                        src,
                        RX.at[i, q - 1, :, span, rows],
                        xy_s.at[i, g, cls, 0, q - 1],
                        xy_r.at[i, g, cls, 0, q - 1],
                        peers[cls][q],
                    ),
                )

    def scatter2(i, g):
        for cls, lo, n, r, m in PARTS[i, g]:
            span, rows = pl.ds(lo, n), pl.ds(r, m)
            total = T[i, x, :, span, rows] if cls == 0 else T[i, :, y, span, rows]
            for q in (1, 2, 3):
                arrive("scatter", i, g, cls, 0, q)
                total = total + RX[i, q - 1, :, span, rows]
            U[i, :, span, rows] = total
            for q in (1, 2, 3):
                at = lax.rem(y + q, 4) if cls == 0 else lax.rem(x + q, 4)
                start(
                    ("scatter", i, g, cls, 1, q),
                    copy(
                        U.at[i, at, span, rows],
                        RY.at[i, q - 1, span, rows],
                        xy_s.at[i, g, cls, 1, q - 1],
                        xy_r.at[i, g, cls, 1, q - 1],
                        peers[1 - cls][q],
                    ),
                )

    def scatter3(i, g):
        for cls, lo, n, r, m in PARTS[i, g]:
            span, rows = pl.ds(lo, n), pl.ds(r, m)
            total = U[i, y if cls == 0 else x, span, rows]
            for q in (1, 2, 3):
                arrive("scatter", i, g, cls, 1, q)
                total = total + RY[i, q - 1, span, rows]
            for p in range(n):
                j = lax.rem(z + ORDER[lo + p], 8)
                rows_out[i, j, rows, :] = total[p]

    stores = []

    def store(src, dst):
        c = pltpu.make_async_copy(src, dst, out_s.at[len(stores)])
        c.start()
        stores.append(c)

    def deliver(i):
        one = identity(LANES)
        main = rows_out[i, :, pl.ds(0, PIECE), :].reshape(HALF, LANES)
        tail = rows_out[i, :, pl.ds(PIECE, 8), :]
        tail = jnp.concatenate([tail, tail], axis=1).reshape(HALF, LANES)
        results[i, pl.ds(0, LANES), :] = dot(one, main.astype(BF16), 1, 1).astype(BF16)
        tail = dot(one, tail.astype(BF16), 1, 1)
        low = lax.broadcasted_iota(jnp.int32, (TAIL, HALF), 1) % PIECE < 8
        results[i, pl.ds(LANES, TAIL), :] = jnp.where(low, tail[:TAIL], tail[TAIL:]).astype(BF16)
        store(results.at[i], (out, gt)[i])

    def grad(n, lo, hi):
        a, b = ((0, 1), (0, 2), (1, 0))[n]

        def body(q, carry):
            for h in range(2):
                for e in range(2):
                    p = dot(packed(a, h, q, e, 0, BLOCK), H[b, 2 * q + e], 0, 0)
                    acc[n, h, pl.ds(0, LANES), :] += p[:LANES]
                    acc[n, h, pl.ds(LANES, TAIL), :] += p[LANES + e * TAIL : LANES + (e + 1) * TAIL]
            return carry

        if hi - lo == 1:
            body(lo, 0)
        else:
            lax.fori_loop(lo, hi, body, 0)

    def grad_swap(n):
        gsend[n] = acc[n, other].astype(BF16)
        start(("grad", n), copy(gsend.at[n], ggot.at[n], gr_s.at[n], gr_r.at[n], sibling))
        grads[n, :, mine] = acc[n, k].astype(BF16)

    def grad_end(n):
        arrive("grad", n)
        grads[n, :, theirs] = ggot[n]
        store(grads.at[n], (gg, gu, gd)[n])

    pieces(0)
    pl.semaphore_wait(barrier, 9)
    gather1(0, 0)
    swap_weights()
    gather2(0, 0)
    pieces(1)
    gather1(1, 0)
    gather1(0, 1)
    acc[...] = jnp.zeros_like(acc)
    expand_theirs()
    gather2(1, 0)
    gather3(0, 0)
    gather2(0, 1)
    gather1(1, 1)
    gather4(0, 0)
    step0(0)
    step0(1)
    gather3(1, 0)
    gather2(1, 1)
    step(0, 1)
    step(1, 1)
    gather3(0, 1)
    gather4(1, 0)
    step0(2)
    gather4(0, 1)
    step(0, 2)
    step(1, 2)
    step(2, 1)
    gather3(1, 1)
    step(0, 3)
    step(1, 3)
    gather4(1, 1)
    step(2, 2)
    finish(0)
    finish(1)
    activate()
    relay_step(0, 0)
    step(2, 3)
    relay_step(0, 1)
    finish(2)
    activate_back()
    relay_step(1, 0)
    relay_step(0, 2)
    products(0, 0, 4, 4)
    relay_step(1, 1)
    scatter1(0, 0)
    relay_step(0, 3)
    grad(2, 2, 4)
    relay_step(1, 2)
    products(1, 0, 4, 4)
    relay_end(0)
    products(0, 1, 0, 4)
    scatter2(0, 0)
    scatter1(1, 0)
    scatter1(0, 1)
    relay_step(1, 3)
    products(1, 1, 1, 3)
    grad(2, 0, 2)
    grad_swap(2)
    scatter2(1, 0)
    scatter1(1, 1)
    scatter2(0, 1)
    grad(0, 1, 4)
    grad(1, 1, 4)
    relay_end(1)
    products(1, 2, 0, 1)
    scatter2(1, 1)
    grad(0, 0, 1)
    grad_swap(0)
    scatter1(1, 2)
    grad(1, 0, 1)
    grad_swap(1)
    scatter3(0, 0)
    scatter3(0, 1)
    deliver(0)
    grad_end(2)
    scatter2(1, 2)
    scatter3(1, 0)
    grad_end(0)
    grad_end(1)
    scatter3(1, 1)
    scatter3(1, 2)
    deliver(1)
    for c in stores:
        c.wait()
    for c in started.values():
        c.wait_send()


def hand_over(*refs):
    for i in range(5):
        refs[5 + i][...] = refs[i][...]


def body(tokens, gate_weight, up_weight, down_weight, cotangent):
    n_tok, width = tokens.shape
    hidden = gate_weight.shape[1]
    dma = pltpu.SemaphoreType.DMA
    V = pltpu.VMEM
    act = jax.ShapeDtypeStruct((width, n_tok), BF16)
    weight = jax.ShapeDtypeStruct((width, hidden), BF16)
    shapes = (act, act, weight, weight, weight)
    scratch = [
        V((2, width, n_tok), BF16),
        V((3, width, hidden), BF16),
        V((2, 2, n_tok, LANES), F32),
        V((2, 2, 4, 4, 4, 3 * PIECE, LANES), BF16),
        V((3, 2, width, BLOCK), BF16),
        V((2, 3, 2, 2 * LANES, BLOCK), BF16),
        V((3, 2, 2 * LANES, BLOCK), BF16),
        V((3, 2, 4, BLOCK, BLOCK), BF16),
        V((3, 2, 4, BLOCK, BLOCK), BF16),
        V((2, BLOCK, BLOCK), F32),
        V((3, BLOCK, BLOCK), F32),
        V((3, 8, BLOCK, BLOCK), BF16),
        V((2, 2, 4, 4, 8, 24, LANES), F32),
        V((2, 4, 4, 8, 24, LANES), F32),
        V((2, 4, 4, 8, 24, LANES), F32),
        V((2, 3, 4, 8, 24, LANES), F32),
        V((2, 4, 8, 24, LANES), F32),
        V((2, 3, 8, 24, LANES), F32),
        V((3, 2, width, BLOCK), F32),
        V((3, width, BLOCK), BF16),
        V((3, width, BLOCK), BF16),
        V((3, width, hidden), BF16),
        V((2, 8, 24, LANES), F32),
        V((2, width, n_tok), BF16),
        dma((5,)), dma((5,)),
        dma((3,)), dma((3,)),
        dma((2, 2, 2, 2, 3)), dma((2, 2, 2, 2, 3)),
        dma((2, 2)), dma((2, 2)),
        dma((3, 2, 4)), dma((3, 2, 4)),
        dma((2, 2, 4)), dma((2, 2, 4)),
        dma((2, 3)), dma((2, 3)),
        dma((2, 3, 2, 2, 3)), dma((2, 3, 2, 2, 3)),
        dma((3,)), dma((3,)),
    ]
    anywhere = pl.BlockSpec(memory_space=pl.ANY)
    held = pl.pallas_call(
        kernel,
        out_shape=shapes,
        in_specs=[anywhere] * 5,
        out_specs=(anywhere,) * 5,
        scratch_shapes=scratch,
        name="feed_forward",
        compiler_params=pltpu.CompilerParams(
            collective_id=0, has_side_effects=True, vmem_limit_bytes=56 * 2**20
        ),
    )(tokens.T, gate_weight, up_weight, down_weight.T, cotangent.T)
    vmem = pl.BlockSpec(memory_space=pltpu.VMEM)
    results = pl.pallas_call(
        hand_over,
        out_shape=shapes,
        in_specs=[vmem] * 5,
        out_specs=(vmem,) * 5,
        name="hand_over",
    )(*held)
    return results[0].T, results[1].T, results[2], results[3], results[4].T


def solution(mesh):
    return jax.shard_map(
        body,
        mesh=mesh,
        in_specs=(
            P("col", "row"),
            P("row", "col"),
            P("row", "col"),
            P("col", "row"),
            P("col", "row"),
        ),
        out_specs=(
            P("col", "row"),
            P("col", "row"),
            P("row", "col"),
            P("row", "col"),
            P("col", "row"),
        ),
        check_vma=False,
    )
```

```python
import jax
import jax.numpy as jnp
from jax import lax
from jax.experimental import pallas as pl
from jax.experimental.pallas import tpu as pltpu
from jax.sharding import PartitionSpec as P

MESH = pl.DeviceIdType.MESH
F32 = jnp.float32
BF16 = jnp.bfloat16

ORDER = (4, 3, 5, 0, 2, 1, 6, 7)
PLACE = {d: o for o, d in enumerate(ORDER)}
PIECE = 16
LANES = 128
TAIL = 64
BLOCK = 256
HALF = 128
RIGHTWARD = tuple(PLACE[d] for d in (0, 7, 6, 5, 4))
LEFTWARD = tuple(PLACE[d] for d in (0, 1, 2, 3, 4))
PARTS = (
    (
        (0, 4, 2, 0, 24), (1, 6, 2, 0, 24),
        (0, 1, 1, 0, 24), (1, 2, 1, 0, 24), (0, 3, 1, 0, 16), (1, 3, 1, 16, 8),
        (0, 0, 1, 0, 8), (1, 0, 1, 8, 16),
    ),
    (
        (0, 5, 1, 0, 24), (1, 7, 1, 0, 24), (0, 3, 1, 0, 8), (1, 3, 1, 8, 16),
        (0, 4, 1, 0, 24), (1, 6, 1, 0, 24),
        (0, 1, 1, 0, 24), (1, 2, 1, 0, 24),
        (0, 0, 1, 0, 16), (1, 0, 1, 16, 8),
    ),
)
GROUPS = (((0, 1), (2, 3, 4, 5), (6, 7)), ((0, 1, 2, 3), (4, 5), (6, 7), (8, 9)))


def dot(a, b, ca, cb):
    return lax.dot_general(a, b, (((ca,), (cb,)), ((), ())), preferred_element_type=F32)


def identity(n):
    rows = lax.broadcasted_iota(jnp.int32, (n, n), 0)
    return (rows == lax.broadcasted_iota(jnp.int32, (n, n), 1)).astype(BF16)


def kernel(
    tok, gw, uw, dw, cot,
    out, gt, gg, gu, gd,
    acts, weights, rows_in, X, W, WE, WP, sent, got, part, final, H,
    S, SR, T, RX, U, RY, acc, gsend, ggot, grads, rows_out, results,
    in_s, out_s, w_s, w_r, ag_s, ag_r, fw_s, fw_r, rs_s, rs_r, ga_s, ga_r, sx_s, sx_r, xy_s, xy_r, gr_s, gr_r,
):
    row, col = lax.axis_index("row"), lax.axis_index("col")
    z, k = row // 2, row % 2
    x, y = col // 4, col % 4
    other = 1 - k
    width = gw.shape[0]
    sibling = (z * 2 + other, col)
    right = (lax.rem(z + 1, 8) * 2 + k, col)
    left = (lax.rem(z + 7, 8) * 2 + k, col)
    xpeers = {i: (row, lax.rem(x + i, 4) * 4 + y) for i in (1, 2, 3)}
    ypeers = {i: (row, x * 4 + lax.rem(y + i, 4)) for i in (1, 2, 3)}
    peers = (xpeers, ypeers)

    def copy(src, dst, s, r, device):
        return pltpu.make_async_remote_copy(
            src_ref=src, dst_ref=dst, send_sem=s, recv_sem=r, device_id=device, device_id_type=MESH
        )

    started = {}

    def start(key, c):
        c.start()
        started[key] = c

    def arrive(*key):
        started[key].wait_recv()

    sent_off = []

    def settle(but=0):
        for key in list(started)[: len(started) - but]:
            if key not in sent_off:
                started[key].wait_send()
                sent_off.append(key)

    barrier = pltpu.get_barrier_semaphore()
    for device in [sibling, right, left, *xpeers.values(), *ypeers.values()]:
        pl.semaphore_signal(barrier, inc=1, device_id=device, device_id_type=MESH)

    first_half = lax.broadcasted_iota(jnp.int32, (PIECE, LANES), 1) < TAIL
    loads = [
        pltpu.make_async_copy(src, dst, in_s.at[i])
        for i, (src, dst) in enumerate(
            ((tok, acts.at[0]), (cot, acts.at[1]), (gw, weights.at[0]), (uw, weights.at[1]), (dw, weights.at[2]))
        )
    ]
    for c in loads:
        c.start()

    def pieces(a):
        loads[a].wait()
        one = identity(HALF)
        tails = acts[a, pl.ds(LANES, TAIL), :]
        rows_in[a, 0] = dot(one, acts[a, pl.ds(0, LANES), :], 1, 1)
        rows_in[a, 1] = dot(one, jnp.concatenate([tails, tails], axis=0), 1, 1)
        for q in range(4):
            at = [pl.ds(pl.multiple_of(lax.rem(z + ORDER[2 * q + e], 8) * PIECE, PIECE), PIECE) for e in range(2)]
            for e in range(2):
                X[a, k, x, y, q, pl.ds(e * PIECE, PIECE), :] = rows_in[a, 0, at[e], :].astype(BF16)
            X[a, k, x, y, q, pl.ds(2 * PIECE, PIECE), :] = jnp.where(
                first_half, rows_in[a, 1, at[0], :], rows_in[a, 1, at[1], :]
            ).astype(BF16)

    def gather1(a, c):
        for cls in range(2):
            ref = X.at[a, k, x, y, 2 * c + cls]
            for i in (1, 2, 3):
                start(
                    ("gather", a, c, cls, 0, i),
                    copy(ref, ref, ag_s.at[a, c, cls, 0, i - 1], ag_r.at[a, c, cls, 0, i - 1], peers[cls][i]),
                )

    def gather2(a, c):
        for cls in range(2):
            q = 2 * c + cls
            for i in (1, 2, 3):
                arrive("gather", a, c, cls, 0, i)
            ref = X.at[a, k, :, y, q] if cls == 0 else X.at[a, k, x, :, q]
            for i in (1, 2, 3):
                start(
                    ("gather", a, c, cls, 1, i),
                    copy(ref, ref, ag_s.at[a, c, cls, 1, i - 1], ag_r.at[a, c, cls, 1, i - 1], peers[1 - cls][i]),
                )

    def gather3(a, c):
        for cls in range(2):
            for i in (1, 2, 3):
                arrive("gather", a, c, cls, 1, i)
        ref = X.at[a, k, :, :, pl.ds(2 * c, 2)]
        start(("pair", a, c), copy(ref, ref, fw_s.at[a, c], fw_r.at[a, c], sibling))

    def gather4(a, c):
        arrive("pair", a, c)

    mine = pl.ds(pl.multiple_of(k * BLOCK, BLOCK), BLOCK)
    theirs = pl.ds(pl.multiple_of(other * BLOCK, BLOCK), BLOCK)

    def swap_weights():
        for i in range(3):
            loads[2 + i].wait()
            start(("weight", i), copy(weights.at[i, :, theirs], W.at[i, k], w_s.at[i], w_r.at[i], sibling))
        for i in range(3):
            W[i, k] = weights[i, :, mine]
            expand(i, k)

    def expand(i, h):
        main, tail = W[i, h, pl.ds(0, LANES), :], W[i, h, pl.ds(LANES, TAIL), :]
        none = jnp.zeros_like(tail)
        for e in range(2):
            WE[e, i, h, pl.ds(0, LANES), :] = main
            WE[e, i, h, pl.ds(LANES + e * TAIL, TAIL), :] = tail
            WE[e, i, h, pl.ds(LANES + (1 - e) * TAIL, TAIL), :] = none
        WP[i, h, pl.ds(0, LANES), :] = main
        for e in range(2):
            WP[i, h, pl.ds(LANES + e * TAIL, TAIL), :] = tail

    def expand_theirs():
        for i in range(3):
            arrive("weight", i)
            expand(i, other)

    def packed(a, h, q, e, first, rows):
        span = pl.ds(first, rows // 64)
        main = X[a, h, span, :, q, pl.ds(e * PIECE, PIECE), :].reshape(rows, LANES)
        tail = X[a, h, span, :, q, pl.ds(2 * PIECE, PIECE), :].reshape(rows, LANES)
        return jnp.concatenate([main, tail], axis=1)

    def local(a, o, first, rows):
        total = None
        for h in range(2):
            p = dot(packed(a // 2, h, o // 2, o % 2, first, rows), WE[o % 2, a, h], 1, 0)
            total = p if total is None else total + p
        return total

    def half(dr):
        return pl.ds(HALF * dr, HALF)

    def chain(a, dr, s, rows):
        start(
            ("chain", a, dr, s),
            copy(
                sent.at[a, dr, s, rows],
                got.at[a, dr, s, rows],
                rs_s.at[a, dr, s],
                rs_r.at[a, dr, s],
                (right, left)[dr],
            ),
        )

    def step0(a):
        for dr in range(2):
            sent[a, dr, 0, half(dr), :] = local(a, PLACE[4], 2 * dr, HALF).astype(BF16)
            chain(a, dr, 0, half(dr))

    def step(a, s):
        for dr in range(2):
            part[dr] = local(a, PLACE[(4 - s, 4 + s)[dr]], 0, BLOCK)
        for dr in range(2):
            arrive("chain", a, dr, s - 1)
            if s == 1:
                sent[a, dr, s, half(dr), :] = (part[dr, half(dr), :] + got[a, dr, 0, half(dr), :].astype(F32)).astype(BF16)
                sent[a, dr, s, half(1 - dr), :] = part[dr, half(1 - dr), :].astype(BF16)
            else:
                sent[a, dr, s] = (part[dr] + got[a, dr, s - 1].astype(F32)).astype(BF16)
            chain(a, dr, s, pl.ds(0, BLOCK))

    def finish(a):
        final[a] = local(a, PLACE[0], 0, BLOCK)
        for dr in range(2):
            arrive("chain", a, dr, 3)
        final[a] += got[a, 0, 3].astype(F32) + got[a, 1, 3].astype(F32)

    def relay_step(m, s):
        for dr in range(2):
            places = (RIGHTWARD, LEFTWARD)[dr]
            rows = half(dr) if s == 3 else pl.ds(0, BLOCK)
            if s > 0:
                arrive("relay", m, dr, s - 1)
            start(
                ("relay", m, dr, s),
                copy(
                    H.at[m, places[s], rows],
                    H.at[m, places[s + 1], rows],
                    ga_s.at[m, dr, s],
                    ga_r.at[m, dr, s],
                    (right, left)[dr],
                ),
            )

    def relay_end(m):
        for dr in range(2):
            arrive("relay", m, dr, 3)

    def activate():
        gate, up = final[0], final[1]
        H[0, PLACE[0]] = ((gate * jax.nn.sigmoid(gate)) * up).astype(BF16)

    def activate_back():
        gate, up, gh = final[0], final[1], final[2]
        sigma = jax.nn.sigmoid(gate)
        H[1, PLACE[0]] = (gh * up * sigma * (1.0 + gate * (1.0 - sigma))).astype(BF16)
        H[2, PLACE[0]] = (gh * (gate * sigma)).astype(BF16)

    def product(i, lo, n):
        def body(o, carry):
            for h in range(2):
                if i == 0:
                    p = dot(H[0, o], WP[2, h], 1, 1)
                else:
                    p = dot(H[1, o], WP[0, h], 1, 1) + dot(H[2, o], WP[1, h], 1, 1)
                S[i, h, :, :, o, pl.ds(0, PIECE), :] = p[:, :LANES].reshape(4, 4, PIECE, LANES)
                tail = p[:, LANES:].reshape(4, 4, PIECE, LANES)
                low = lax.broadcasted_iota(jnp.int32, (4, 4, 8, LANES), 3) < TAIL
                S[i, h, :, :, o, pl.ds(PIECE, 8), :] = jnp.where(low, tail[:, :, :8], tail[:, :, 8:])
            return carry

        if n == 1:
            body(lo, 0)
        else:
            lax.fori_loop(lo, lo + n, body, 0)

    def part_of(i, u):
        cls, lo, n, r, m = PARTS[i][u]
        return cls, lo, n, pl.ds(lo, n), pl.ds(r, m)

    def products(i, g):
        for lo, n in dict.fromkeys(PARTS[i][u][1:3] for u in GROUPS[i][g]):
            product(i, lo, n)
            for u in GROUPS[i][g]:
                if PARTS[i][u][1] == lo:
                    cls, lo, n, span, rows = part_of(i, u)
                    start(
                        ("cores", i, u),
                        copy(
                            S.at[i, other, :, :, span, rows],
                            SR.at[i, :, :, span, rows],
                            sx_s.at[i, u],
                            sx_r.at[i, u],
                            sibling,
                        ),
                    )

    def scatter1(i, g):
        for u in GROUPS[i][g]:
            cls, lo, n, span, rows = part_of(i, u)
            arrive("cores", i, u)
            T[i, :, :, span, rows] = S[i, k, :, :, span, rows] + SR[i, :, :, span, rows]
            for q in (1, 2, 3):
                if cls == 0:
                    src = T.at[i, lax.rem(x + q, 4), :, span, rows]
                else:
                    src = T.at[i, :, lax.rem(y + q, 4), span, rows]
                start(
                    ("scatter", i, u, 0, q),
                    copy(
                        src,
                        RX.at[i, q - 1, :, span, rows],
                        xy_s.at[i, u, 0, q - 1],
                        xy_r.at[i, u, 0, q - 1],
                        peers[cls][q],
                    ),
                )

    def scatter2(i, g):
        for u in GROUPS[i][g]:
            cls, lo, n, span, rows = part_of(i, u)
            total = T[i, x, :, span, rows] if cls == 0 else T[i, :, y, span, rows]
            for q in (1, 2, 3):
                arrive("scatter", i, u, 0, q)
                total = total + RX[i, q - 1, :, span, rows]
            U[i, :, span, rows] = total
            for q in (1, 2, 3):
                at = lax.rem(y + q, 4) if cls == 0 else lax.rem(x + q, 4)
                start(
                    ("scatter", i, u, 1, q),
                    copy(
                        U.at[i, at, span, rows],
                        RY.at[i, q - 1, span, rows],
                        xy_s.at[i, u, 1, q - 1],
                        xy_r.at[i, u, 1, q - 1],
                        peers[1 - cls][q],
                    ),
                )

    def scatter3(i, g):
        for u in GROUPS[i][g]:
            cls, lo, n, span, rows = part_of(i, u)
            total = U[i, y if cls == 0 else x, span, rows]
            for q in (1, 2, 3):
                arrive("scatter", i, u, 1, q)
                total = total + RY[i, q - 1, span, rows]
            for p in range(n):
                rows_out[i, lax.rem(z + ORDER[lo + p], 8), rows, :] = total[p]

    stores = []

    def store(src, dst):
        c = pltpu.make_async_copy(src, dst, out_s.at[len(stores)])
        c.start()
        stores.append(c)

    def deliver(i):
        one = identity(LANES)
        main = rows_out[i, :, pl.ds(0, PIECE), :].reshape(HALF, LANES)
        tail = rows_out[i, :, pl.ds(PIECE, 8), :]
        tail = jnp.concatenate([tail, tail], axis=1).reshape(HALF, LANES)
        results[i, pl.ds(0, LANES), :] = dot(one, main.astype(BF16), 1, 1).astype(BF16)
        tail = dot(one, tail.astype(BF16), 1, 1)
        low = lax.broadcasted_iota(jnp.int32, (TAIL, HALF), 1) % PIECE < 8
        results[i, pl.ds(LANES, TAIL), :] = jnp.where(low, tail[:TAIL], tail[TAIL:]).astype(BF16)
        store(results.at[i], (out, gt)[i])

    def grad(n, lo, hi):
        a, b = ((0, 1), (0, 2), (1, 0))[n]

        def body(q, carry):
            for h in range(2):
                for e in range(2):
                    p = dot(packed(a, h, q, e, 0, BLOCK), H[b, 2 * q + e], 0, 0)
                    acc[n, h, pl.ds(0, LANES), :] += p[:LANES]
                    acc[n, h, pl.ds(LANES, TAIL), :] += p[LANES + e * TAIL : LANES + (e + 1) * TAIL]
            return carry

        if hi - lo == 1:
            body(lo, 0)
        else:
            lax.fori_loop(lo, hi, body, 0)

    def grad_swap(n):
        gsend[n] = acc[n, other].astype(BF16)
        start(("grad", n), copy(gsend.at[n], ggot.at[n], gr_s.at[n], gr_r.at[n], sibling))
        grads[n, :, mine] = acc[n, k].astype(BF16)

    def grad_end(n):
        arrive("grad", n)
        grads[n, :, theirs] = ggot[n]
        store(grads.at[n], (gg, gu, gd)[n])

    pieces(0)
    pl.semaphore_wait(barrier, 9)
    gather1(0, 0)
    swap_weights()
    gather2(0, 0)
    pieces(1)
    gather1(1, 0)
    gather1(0, 1)
    acc[...] = jnp.zeros_like(acc)
    expand_theirs()
    gather2(1, 0)
    gather3(0, 0)
    gather2(0, 1)
    gather1(1, 1)
    gather4(0, 0)
    step0(0)
    step0(1)
    gather3(1, 0)
    gather2(1, 1)
    step(0, 1)
    step(1, 1)
    gather3(0, 1)
    gather4(1, 0)
    step0(2)
    gather4(0, 1)
    step(0, 2)
    step(1, 2)
    step(2, 1)
    gather3(1, 1)
    step(0, 3)
    step(1, 3)
    gather4(1, 1)
    step(2, 2)
    finish(0)
    finish(1)
    activate()
    relay_step(0, 0)
    step(2, 3)
    relay_step(0, 1)
    finish(2)
    activate_back()
    relay_step(1, 0)
    relay_step(2, 0)
    relay_step(0, 2)
    products(0, 0)
    relay_step(1, 1)
    scatter1(0, 0)
    relay_step(2, 1)
    products(1, 0)
    grad(2, 2, 4)
    relay_step(0, 3)
    products(0, 1)
    scatter1(1, 0)
    scatter2(0, 0)
    relay_step(1, 2)
    scatter1(0, 1)
    relay_step(2, 2)
    products(1, 1)
    scatter2(1, 0)
    relay_end(0)
    products(0, 2)
    scatter1(1, 1)
    grad(2, 0, 2)
    grad_swap(2)
    scatter1(0, 2)
    relay_step(1, 3)
    scatter2(0, 1)
    relay_step(2, 3)
    settle(24)
    products(1, 2)
    scatter2(1, 1)
    scatter2(0, 2)
    grad(0, 1, 4)
    scatter1(1, 2)
    grad(1, 1, 4)
    relay_end(1)
    relay_end(2)
    products(1, 3)
    grad(0, 0, 1)
    grad_swap(0)
    scatter1(1, 3)
    grad(1, 0, 1)
    grad_swap(1)
    scatter2(1, 2)
    scatter3(0, 0)
    scatter3(0, 1)
    scatter3(0, 2)
    deliver(0)
    scatter2(1, 3)
    grad_end(2)
    scatter3(1, 0)
    scatter3(1, 1)
    grad_end(0)
    grad_end(1)
    settle(8)
    scatter3(1, 2)
    scatter3(1, 3)
    deliver(1)
    for c in stores:
        c.wait()
    settle()


def hand_over(*refs):
    held, results, kept, sems = refs[:5], refs[5:10], refs[10:15], refs[15]
    loads = [pltpu.make_async_copy(held[i], kept[i], sems.at[0, i]) for i in range(5)]
    stores = [pltpu.make_async_copy(kept[i], results[i], sems.at[1, i]) for i in range(5)]
    for c in loads:
        c.start()
    for load, store in zip(loads, stores):
        load.wait()
        store.start()
    for c in stores:
        c.wait()


def body(tokens, gate_weight, up_weight, down_weight, cotangent):
    n_tok, width = tokens.shape
    hidden = gate_weight.shape[1]
    dma = pltpu.SemaphoreType.DMA
    V = pltpu.VMEM
    act = jax.ShapeDtypeStruct((width, n_tok), BF16)
    weight = jax.ShapeDtypeStruct((width, hidden), BF16)
    shapes = (act, act, weight, weight, weight)
    scratch = [
        V((2, width, n_tok), BF16),
        V((3, width, hidden), BF16),
        V((2, 2, n_tok, LANES), F32),
        V((2, 2, 4, 4, 4, 3 * PIECE, LANES), BF16),
        V((3, 2, width, BLOCK), BF16),
        V((2, 3, 2, 2 * LANES, BLOCK), BF16),
        V((3, 2, 2 * LANES, BLOCK), BF16),
        V((3, 2, 4, BLOCK, BLOCK), BF16),
        V((3, 2, 4, BLOCK, BLOCK), BF16),
        V((2, BLOCK, BLOCK), F32),
        V((3, BLOCK, BLOCK), F32),
        V((3, 8, BLOCK, BLOCK), BF16),
        V((2, 2, 4, 4, 8, 24, LANES), F32),
        V((2, 4, 4, 8, 24, LANES), F32),
        V((2, 4, 4, 8, 24, LANES), F32),
        V((2, 3, 4, 8, 24, LANES), F32),
        V((2, 4, 8, 24, LANES), F32),
        V((2, 3, 8, 24, LANES), F32),
        V((3, 2, width, BLOCK), F32),
        V((3, width, BLOCK), BF16),
        V((3, width, BLOCK), BF16),
        V((3, width, hidden), BF16),
        V((2, 8, 24, LANES), F32),
        V((2, width, n_tok), BF16),
        dma((5,)), dma((5,)),
        dma((3,)), dma((3,)),
        dma((2, 2, 2, 2, 3)), dma((2, 2, 2, 2, 3)),
        dma((2, 2)), dma((2, 2)),
        dma((3, 2, 4)), dma((3, 2, 4)),
        dma((3, 2, 4)), dma((3, 2, 4)),
        dma((2, 10)), dma((2, 10)),
        dma((2, 10, 2, 3)), dma((2, 10, 2, 3)),
        dma((3,)), dma((3,)),
    ]
    anywhere = pl.BlockSpec(memory_space=pl.ANY)
    held = pl.pallas_call(
        kernel,
        out_shape=shapes,
        in_specs=[anywhere] * 5,
        out_specs=(anywhere,) * 5,
        scratch_shapes=scratch,
        name="feed_forward",
        compiler_params=pltpu.CompilerParams(
            collective_id=0, has_side_effects=True, vmem_limit_bytes=56 * 2**20
        ),
    )(tokens.T, gate_weight, up_weight, down_weight.T, cotangent.T)
    results = pl.pallas_call(
        hand_over,
        out_shape=shapes,
        in_specs=[anywhere] * 5,
        out_specs=(anywhere,) * 5,
        scratch_shapes=[V(v.shape, BF16) for v in shapes] + [dma((2, 5))],
        name="hand_over",
        compiler_params=pltpu.CompilerParams(vmem_limit_bytes=60 * 2**20),
    )(*held)
    return results[0].T, results[1].T, results[2], results[3], results[4].T


def solution(mesh):
    return jax.shard_map(
        body,
        mesh=mesh,
        in_specs=(
            P("col", "row"),
            P("row", "col"),
            P("row", "col"),
            P("col", "row"),
            P("col", "row"),
        ),
        out_specs=(
            P("col", "row"),
            P("col", "row"),
            P("row", "col"),
            P("row", "col"),
            P("col", "row"),
        ),
        check_vma=False,
    )
```

```python
import jax
import jax.numpy as jnp
from jax import lax
from jax.experimental import pallas as pl
from jax.experimental.pallas import tpu as pltpu
from jax.sharding import PartitionSpec as P

MESH = pl.DeviceIdType.MESH
F32 = jnp.float32
BF16 = jnp.bfloat16

ORDER = (4, 3, 5, 0, 2, 1, 6, 7)
PLACE = {d: o for o, d in enumerate(ORDER)}
PIECE = 16
LANES = 128
TAIL = 64
BLOCK = 256
HALF = 128
RIGHTWARD = tuple(PLACE[d] for d in (0, 7, 6, 5, 4))
LEFTWARD = tuple(PLACE[d] for d in (0, 1, 2, 3, 4))
PARTS = (
    (
        (0, 4, 2, 0, 24), (1, 6, 2, 0, 24),
        (0, 1, 1, 0, 24), (1, 2, 1, 0, 24), (0, 3, 1, 0, 16), (1, 3, 1, 16, 8),
        (0, 0, 1, 0, 8), (1, 0, 1, 8, 16),
    ),
    (
        (0, 5, 1, 0, 24), (1, 7, 1, 0, 24), (0, 3, 1, 0, 8), (1, 3, 1, 8, 16),
        (0, 4, 1, 0, 24), (1, 6, 1, 0, 24),
        (0, 1, 1, 0, 24), (1, 2, 1, 0, 24),
        (0, 0, 1, 0, 16), (1, 0, 1, 16, 8),
    ),
)
GROUPS = (((0, 1), (2, 3, 4, 5), (6, 7)), ((0, 1, 2, 3), (4, 5), (6, 7), (8, 9)))


def dot(a, b, ca, cb):
    return lax.dot_general(a, b, (((ca,), (cb,)), ((), ())), preferred_element_type=F32)


def identity(n):
    rows = lax.broadcasted_iota(jnp.int32, (n, n), 0)
    return (rows == lax.broadcasted_iota(jnp.int32, (n, n), 1)).astype(BF16)


def kernel(
    tok, gw, uw, dw, cot,
    out, gt, gg, gu, gd,
    acts, weights, rows_in, X, W, WE, WP, sent, got, part, final, H,
    S, SR, T, RX, U, RY, acc, gsend, ggot, grads, rows_out, results,
    in_s, out_s, w_s, w_r, ag_s, ag_r, fw_s, fw_r, rs_s, rs_r, ga_s, ga_r, sx_s, sx_r, xy_s, xy_r, gr_s, gr_r,
):
    row, col = lax.axis_index("row"), lax.axis_index("col")
    z, k = row // 2, row % 2
    x, y = col // 4, col % 4
    other = 1 - k
    width = gw.shape[0]
    sibling = (z * 2 + other, col)
    right = (lax.rem(z + 1, 8) * 2 + k, col)
    left = (lax.rem(z + 7, 8) * 2 + k, col)
    xpeers = {i: (row, lax.rem(x + i, 4) * 4 + y) for i in (1, 2, 3)}
    ypeers = {i: (row, x * 4 + lax.rem(y + i, 4)) for i in (1, 2, 3)}
    peers = (xpeers, ypeers)

    def copy(src, dst, s, r, device):
        return pltpu.make_async_remote_copy(
            src_ref=src, dst_ref=dst, send_sem=s, recv_sem=r, device_id=device, device_id_type=MESH
        )

    started = {}

    def start(key, c):
        c.start()
        started[key] = c

    def arrive(*key):
        started[key].wait_recv()

    sent_off = []

    def settle(but=0):
        for key in list(started)[: len(started) - but]:
            if key not in sent_off:
                started[key].wait_send()
                sent_off.append(key)

    barrier = pltpu.get_barrier_semaphore()
    for device in [sibling, right, left, *xpeers.values(), *ypeers.values()]:
        pl.semaphore_signal(barrier, inc=1, device_id=device, device_id_type=MESH)

    first_half = lax.broadcasted_iota(jnp.int32, (PIECE, LANES), 1) < TAIL
    loads = [
        pltpu.make_async_copy(src, dst, in_s.at[i])
        for i, (src, dst) in enumerate(
            ((tok, acts.at[0]), (cot, acts.at[1]), (gw, weights.at[0]), (uw, weights.at[1]), (dw, weights.at[2]))
        )
    ]
    for c in loads:
        c.start()

    def pieces(a):
        loads[a].wait()
        one = identity(HALF)
        tails = acts[a, pl.ds(LANES, TAIL), :]
        rows_in[a, 0] = dot(one, acts[a, pl.ds(0, LANES), :], 1, 1)
        rows_in[a, 1] = dot(one, jnp.concatenate([tails, tails], axis=0), 1, 1)
        for q in range(4):
            at = [pl.ds(pl.multiple_of(lax.rem(z + ORDER[2 * q + e], 8) * PIECE, PIECE), PIECE) for e in range(2)]
            for e in range(2):
                X[a, k, x, y, q, pl.ds(e * PIECE, PIECE), :] = rows_in[a, 0, at[e], :].astype(BF16)
            X[a, k, x, y, q, pl.ds(2 * PIECE, PIECE), :] = jnp.where(
                first_half, rows_in[a, 1, at[0], :], rows_in[a, 1, at[1], :]
            ).astype(BF16)

    def gather1(a, c):
        for cls in range(2):
            ref = X.at[a, k, x, y, 2 * c + cls]
            for i in (1, 2, 3):
                start(
                    ("gather", a, c, cls, 0, i),
                    copy(ref, ref, ag_s.at[a, c, cls, 0, i - 1], ag_r.at[a, c, cls, 0, i - 1], peers[cls][i]),
                )

    def gather2(a, c):
        for cls in range(2):
            q = 2 * c + cls
            for i in (1, 2, 3):
                arrive("gather", a, c, cls, 0, i)
            ref = X.at[a, k, :, y, q] if cls == 0 else X.at[a, k, x, :, q]
            for i in (1, 2, 3):
                start(
                    ("gather", a, c, cls, 1, i),
                    copy(ref, ref, ag_s.at[a, c, cls, 1, i - 1], ag_r.at[a, c, cls, 1, i - 1], peers[1 - cls][i]),
                )

    def gather3(a, c):
        for cls in range(2):
            for i in (1, 2, 3):
                arrive("gather", a, c, cls, 1, i)
            ref = X.at[a, k, :, :, 2 * c + cls]
            start(("pair", a, c, cls), copy(ref, ref, fw_s.at[a, c, cls], fw_r.at[a, c, cls], sibling))

    def gather4(a, c, cls):
        arrive("pair", a, c, cls)

    mine = pl.ds(pl.multiple_of(k * BLOCK, BLOCK), BLOCK)
    theirs = pl.ds(pl.multiple_of(other * BLOCK, BLOCK), BLOCK)

    def swap_weights():
        for i in range(3):
            loads[2 + i].wait()
            start(("weight", i), copy(weights.at[i, :, theirs], W.at[i, k], w_s.at[i], w_r.at[i], sibling))
        for i in range(3):
            W[i, k] = weights[i, :, mine]
            expand(i, k)

    def expand(i, h):
        main, tail = W[i, h, pl.ds(0, LANES), :], W[i, h, pl.ds(LANES, TAIL), :]
        none = jnp.zeros_like(tail)
        for e in range(2):
            WE[e, i, h, pl.ds(0, LANES), :] = main
            WE[e, i, h, pl.ds(LANES + e * TAIL, TAIL), :] = tail
            WE[e, i, h, pl.ds(LANES + (1 - e) * TAIL, TAIL), :] = none
        WP[i, h, pl.ds(0, LANES), :] = main
        for e in range(2):
            WP[i, h, pl.ds(LANES + e * TAIL, TAIL), :] = tail

    def expand_theirs():
        for i in range(3):
            arrive("weight", i)
            expand(i, other)

    def packed(a, h, q, e, first, rows):
        span = pl.ds(first, rows // 64)
        main = X[a, h, span, :, q, pl.ds(e * PIECE, PIECE), :].reshape(rows, LANES)
        tail = X[a, h, span, :, q, pl.ds(2 * PIECE, PIECE), :].reshape(rows, LANES)
        return jnp.concatenate([main, tail], axis=1)

    def local(a, o, first, rows):
        total = None
        for h in range(2):
            p = dot(packed(a // 2, h, o // 2, o % 2, first, rows), WE[o % 2, a, h], 1, 0)
            total = p if total is None else total + p
        return total

    def half(dr):
        return pl.ds(HALF * dr, HALF)

    def chain(a, dr, s, rows):
        start(
            ("chain", a, dr, s),
            copy(
                sent.at[a, dr, s, rows],
                got.at[a, dr, s, rows],
                rs_s.at[a, dr, s],
                rs_r.at[a, dr, s],
                (right, left)[dr],
            ),
        )

    def step0(a):
        for dr in range(2):
            sent[a, dr, 0, half(dr), :] = local(a, PLACE[4], 2 * dr, HALF).astype(BF16)
            chain(a, dr, 0, half(dr))

    def step(a, s):
        for dr in range(2):
            part[dr] = local(a, PLACE[(4 - s, 4 + s)[dr]], 0, BLOCK)
        for dr in range(2):
            arrive("chain", a, dr, s - 1)
            if s == 1:
                sent[a, dr, s, half(dr), :] = (part[dr, half(dr), :] + got[a, dr, 0, half(dr), :].astype(F32)).astype(BF16)
                sent[a, dr, s, half(1 - dr), :] = part[dr, half(1 - dr), :].astype(BF16)
            else:
                sent[a, dr, s] = (part[dr] + got[a, dr, s - 1].astype(F32)).astype(BF16)
            chain(a, dr, s, pl.ds(0, BLOCK))

    def finish(a):
        final[a] = local(a, PLACE[0], 0, BLOCK)
        for dr in range(2):
            arrive("chain", a, dr, 3)
        final[a] += got[a, 0, 3].astype(F32) + got[a, 1, 3].astype(F32)

    def relay_step(m, s):
        for dr in range(2):
            places = (RIGHTWARD, LEFTWARD)[dr]
            rows = half(dr) if s == 3 else pl.ds(0, BLOCK)
            if s > 0:
                arrive("relay", m, dr, s - 1)
            start(
                ("relay", m, dr, s),
                copy(
                    H.at[m, places[s], rows],
                    H.at[m, places[s + 1], rows],
                    ga_s.at[m, dr, s],
                    ga_r.at[m, dr, s],
                    (right, left)[dr],
                ),
            )

    def relay_end(m):
        for dr in range(2):
            arrive("relay", m, dr, 3)

    def activate():
        gate, up = final[0], final[1]
        H[0, PLACE[0]] = ((gate * jax.nn.sigmoid(gate)) * up).astype(BF16)

    def activate_back():
        gate, up, gh = final[0], final[1], final[2]
        sigma = jax.nn.sigmoid(gate)
        H[1, PLACE[0]] = (gh * up * sigma * (1.0 + gate * (1.0 - sigma))).astype(BF16)
        H[2, PLACE[0]] = (gh * (gate * sigma)).astype(BF16)

    def product(i, lo, n):
        def body(o, carry):
            for h in range(2):
                if i == 0:
                    p = dot(H[0, o], WP[2, h], 1, 1)
                else:
                    p = dot(H[1, o], WP[0, h], 1, 1) + dot(H[2, o], WP[1, h], 1, 1)
                S[i, h, :, :, o, pl.ds(0, PIECE), :] = p[:, :LANES].reshape(4, 4, PIECE, LANES)
                tail = p[:, LANES:].reshape(4, 4, PIECE, LANES)
                low = lax.broadcasted_iota(jnp.int32, (4, 4, 8, LANES), 3) < TAIL
                S[i, h, :, :, o, pl.ds(PIECE, 8), :] = jnp.where(low, tail[:, :, :8], tail[:, :, 8:])
            return carry

        if n == 1:
            body(lo, 0)
        else:
            lax.fori_loop(lo, lo + n, body, 0)

    def part_of(i, u):
        cls, lo, n, r, m = PARTS[i][u]
        return cls, lo, n, pl.ds(lo, n), pl.ds(r, m)

    def products(i, g):
        for lo, n in dict.fromkeys(PARTS[i][u][1:3] for u in GROUPS[i][g]):
            product(i, lo, n)
            for u in GROUPS[i][g]:
                if PARTS[i][u][1] == lo:
                    cls, lo, n, span, rows = part_of(i, u)
                    start(
                        ("cores", i, u),
                        copy(
                            S.at[i, other, :, :, span, rows],
                            SR.at[i, :, :, span, rows],
                            sx_s.at[i, u],
                            sx_r.at[i, u],
                            sibling,
                        ),
                    )

    def scatter1(i, g):
        for u in GROUPS[i][g]:
            cls, lo, n, span, rows = part_of(i, u)
            arrive("cores", i, u)
            T[i, :, :, span, rows] = S[i, k, :, :, span, rows] + SR[i, :, :, span, rows]
            for q in (1, 2, 3):
                if cls == 0:
                    src = T.at[i, lax.rem(x + q, 4), :, span, rows]
                else:
                    src = T.at[i, :, lax.rem(y + q, 4), span, rows]
                start(
                    ("scatter", i, u, 0, q),
                    copy(
                        src,
                        RX.at[i, q - 1, :, span, rows],
                        xy_s.at[i, u, 0, q - 1],
                        xy_r.at[i, u, 0, q - 1],
                        peers[cls][q],
                    ),
                )

    def scatter2(i, g):
        for u in GROUPS[i][g]:
            cls, lo, n, span, rows = part_of(i, u)
            total = T[i, x, :, span, rows] if cls == 0 else T[i, :, y, span, rows]
            for q in (1, 2, 3):
                arrive("scatter", i, u, 0, q)
                total = total + RX[i, q - 1, :, span, rows]
            U[i, :, span, rows] = total
            for q in (1, 2, 3):
                at = lax.rem(y + q, 4) if cls == 0 else lax.rem(x + q, 4)
                start(
                    ("scatter", i, u, 1, q),
                    copy(
                        U.at[i, at, span, rows],
                        RY.at[i, q - 1, span, rows],
                        xy_s.at[i, u, 1, q - 1],
                        xy_r.at[i, u, 1, q - 1],
                        peers[1 - cls][q],
                    ),
                )

    def scatter3(i, g):
        for u in GROUPS[i][g]:
            cls, lo, n, span, rows = part_of(i, u)
            total = U[i, y if cls == 0 else x, span, rows]
            for q in (1, 2, 3):
                arrive("scatter", i, u, 1, q)
                total = total + RY[i, q - 1, span, rows]
            for p in range(n):
                rows_out[i, lax.rem(z + ORDER[lo + p], 8), rows, :] = total[p]

    stores = []

    def store(src, dst):
        c = pltpu.make_async_copy(src, dst, out_s.at[len(stores)])
        c.start()
        stores.append(c)

    def deliver(i):
        one = identity(LANES)
        main = rows_out[i, :, pl.ds(0, PIECE), :].reshape(HALF, LANES)
        tail = rows_out[i, :, pl.ds(PIECE, 8), :]
        tail = jnp.concatenate([tail, tail], axis=1).reshape(HALF, LANES)
        results[i, pl.ds(0, LANES), :] = dot(one, main.astype(BF16), 1, 1).astype(BF16)
        tail = dot(one, tail.astype(BF16), 1, 1)
        low = lax.broadcasted_iota(jnp.int32, (TAIL, HALF), 1) % PIECE < 8
        results[i, pl.ds(LANES, TAIL), :] = jnp.where(low, tail[:TAIL], tail[TAIL:]).astype(BF16)
        store(results.at[i], (out, gt)[i])

    def grad(n, lo, hi):
        a, b = ((0, 1), (0, 2), (1, 0))[n]

        def body(q, carry):
            for h in range(2):
                for e in range(2):
                    p = dot(packed(a, h, q, e, 0, BLOCK), H[b, 2 * q + e], 0, 0)
                    acc[n, h, pl.ds(0, LANES), :] += p[:LANES]
                    acc[n, h, pl.ds(LANES, TAIL), :] += p[LANES + e * TAIL : LANES + (e + 1) * TAIL]
            return carry

        if hi - lo == 1:
            body(lo, 0)
        else:
            lax.fori_loop(lo, hi, body, 0)

    def grad_swap(n):
        gsend[n] = acc[n, other].astype(BF16)
        start(("grad", n), copy(gsend.at[n], ggot.at[n], gr_s.at[n], gr_r.at[n], sibling))
        grads[n, :, mine] = acc[n, k].astype(BF16)

    def grad_end(n):
        arrive("grad", n)
        grads[n, :, theirs] = ggot[n]
        store(grads.at[n], (gg, gu, gd)[n])

    pieces(0)
    pl.semaphore_wait(barrier, 9)
    gather1(0, 0)
    swap_weights()
    gather2(0, 0)
    pieces(1)
    gather1(1, 0)
    gather1(0, 1)
    acc[...] = jnp.zeros_like(acc)
    expand_theirs()
    gather3(0, 0)
    gather2(1, 0)
    gather2(0, 1)
    gather1(1, 1)
    gather4(0, 0, 0)
    step0(0)
    step0(1)
    gather4(0, 0, 1)
    gather3(1, 0)
    gather2(1, 1)
    step(0, 1)
    step(1, 1)
    gather3(0, 1)
    gather4(1, 0, 0)
    step0(2)
    gather4(0, 1, 0)
    gather4(0, 1, 1)
    step(0, 2)
    step(1, 2)
    gather4(1, 0, 1)
    step(2, 1)
    gather3(1, 1)
    step(0, 3)
    step(1, 3)
    gather4(1, 1, 0)
    gather4(1, 1, 1)
    step(2, 2)
    finish(0)
    finish(1)
    activate()
    relay_step(0, 0)
    step(2, 3)
    relay_step(0, 1)
    finish(2)
    activate_back()
    relay_step(1, 0)
    relay_step(2, 0)
    relay_step(0, 2)
    products(0, 0)
    relay_step(1, 1)
    scatter1(0, 0)
    relay_step(2, 1)
    products(1, 0)
    grad(2, 2, 4)
    relay_step(0, 3)
    products(0, 1)
    scatter1(1, 0)
    scatter2(0, 0)
    relay_step(1, 2)
    scatter1(0, 1)
    relay_step(2, 2)
    products(1, 1)
    scatter2(1, 0)
    relay_end(0)
    products(0, 2)
    scatter1(1, 1)
    grad(2, 0, 2)
    grad_swap(2)
    scatter1(0, 2)
    relay_step(1, 3)
    scatter2(0, 1)
    relay_step(2, 3)
    settle(24)
    products(1, 2)
    scatter2(1, 1)
    scatter2(0, 2)
    scatter1(1, 2)
    relay_end(1)
    relay_end(2)
    products(1, 3)
    grad(0, 0, 4)
    grad_swap(0)
    scatter1(1, 3)
    scatter2(1, 2)
    grad(1, 0, 4)
    grad_swap(1)
    scatter3(0, 0)
    scatter3(0, 1)
    scatter3(0, 2)
    scatter2(1, 3)
    deliver(0)
    grad_end(2)
    scatter3(1, 0)
    scatter3(1, 1)
    grad_end(0)
    grad_end(1)
    settle(8)
    scatter3(1, 2)
    scatter3(1, 3)
    deliver(1)
    for c in stores:
        c.wait()
    settle()


def hand_over(*refs):
    held, results, kept, sems = refs[:5], refs[5:10], refs[10:15], refs[15]
    loads = [pltpu.make_async_copy(held[i], kept[i], sems.at[0, i]) for i in range(5)]
    stores = [pltpu.make_async_copy(kept[i], results[i], sems.at[1, i]) for i in range(5)]
    for c in loads:
        c.start()
    for load, store in zip(loads, stores):
        load.wait()
        store.start()
    for c in stores:
        c.wait()


def body(tokens, gate_weight, up_weight, down_weight, cotangent):
    n_tok, width = tokens.shape
    hidden = gate_weight.shape[1]
    dma = pltpu.SemaphoreType.DMA
    V = pltpu.VMEM
    act = jax.ShapeDtypeStruct((width, n_tok), BF16)
    weight = jax.ShapeDtypeStruct((width, hidden), BF16)
    shapes = (act, act, weight, weight, weight)
    scratch = [
        V((2, width, n_tok), BF16),
        V((3, width, hidden), BF16),
        V((2, 2, n_tok, LANES), F32),
        V((2, 2, 4, 4, 4, 3 * PIECE, LANES), BF16),
        V((3, 2, width, BLOCK), BF16),
        V((2, 3, 2, 2 * LANES, BLOCK), BF16),
        V((3, 2, 2 * LANES, BLOCK), BF16),
        V((3, 2, 4, BLOCK, BLOCK), BF16),
        V((3, 2, 4, BLOCK, BLOCK), BF16),
        V((2, BLOCK, BLOCK), F32),
        V((3, BLOCK, BLOCK), F32),
        V((3, 8, BLOCK, BLOCK), BF16),
        V((2, 2, 4, 4, 8, 24, LANES), F32),
        V((2, 4, 4, 8, 24, LANES), F32),
        V((2, 4, 4, 8, 24, LANES), F32),
        V((2, 3, 4, 8, 24, LANES), F32),
        V((2, 4, 8, 24, LANES), F32),
        V((2, 3, 8, 24, LANES), F32),
        V((3, 2, width, BLOCK), F32),
        V((3, width, BLOCK), BF16),
        V((3, width, BLOCK), BF16),
        V((3, width, hidden), BF16),
        V((2, 8, 24, LANES), F32),
        V((2, width, n_tok), BF16),
        dma((5,)), dma((5,)),
        dma((3,)), dma((3,)),
        dma((2, 2, 2, 2, 3)), dma((2, 2, 2, 2, 3)),
        dma((2, 2, 2)), dma((2, 2, 2)),
        dma((3, 2, 4)), dma((3, 2, 4)),
        dma((3, 2, 4)), dma((3, 2, 4)),
        dma((2, 10)), dma((2, 10)),
        dma((2, 10, 2, 3)), dma((2, 10, 2, 3)),
        dma((3,)), dma((3,)),
    ]
    anywhere = pl.BlockSpec(memory_space=pl.ANY)
    held = pl.pallas_call(
        kernel,
        out_shape=shapes,
        in_specs=[anywhere] * 5,
        out_specs=(anywhere,) * 5,
        scratch_shapes=scratch,
        name="feed_forward",
        compiler_params=pltpu.CompilerParams(
            collective_id=0, has_side_effects=True, vmem_limit_bytes=56 * 2**20
        ),
    )(tokens.T, gate_weight, up_weight, down_weight.T, cotangent.T)
    results = pl.pallas_call(
        hand_over,
        out_shape=shapes,
        in_specs=[anywhere] * 5,
        out_specs=(anywhere,) * 5,
        scratch_shapes=[V(v.shape, BF16) for v in shapes] + [dma((2, 5))],
        name="hand_over",
        compiler_params=pltpu.CompilerParams(vmem_limit_bytes=60 * 2**20),
    )(*held)
    return results[0].T, results[1].T, results[2], results[3], results[4].T


def solution(mesh):
    return jax.shard_map(
        body,
        mesh=mesh,
        in_specs=(
            P("col", "row"),
            P("row", "col"),
            P("row", "col"),
            P("col", "row"),
            P("col", "row"),
        ),
        out_specs=(
            P("col", "row"),
            P("col", "row"),
            P("row", "col"),
            P("row", "col"),
            P("col", "row"),
        ),
        check_vma=False,
    )
```

```python
import jax
import jax.numpy as jnp
from jax import lax
from jax.experimental import pallas as pl
from jax.experimental.pallas import tpu as pltpu
from jax.sharding import PartitionSpec as P

MESH = pl.DeviceIdType.MESH
F32 = jnp.float32
BF16 = jnp.bfloat16

ORDER = (4, 3, 5, 0, 2, 1, 6, 7)
PLACE = {d: o for o, d in enumerate(ORDER)}
PIECE = 16
LANES = 128
TAIL = 64
BLOCK = 256
HALF = 128
RIGHTWARD = tuple(PLACE[d] for d in (0, 7, 6, 5, 4))
LEFTWARD = tuple(PLACE[d] for d in (0, 1, 2, 3, 4))
PARTS = (
    (
        (0, 4, 2, 0, 24), (1, 6, 2, 0, 24),
        (0, 1, 1, 0, 24), (1, 2, 1, 0, 24), (0, 3, 1, 0, 16), (1, 3, 1, 16, 8),
        (0, 0, 1, 0, 8), (1, 0, 1, 8, 16),
    ),
    (
        (0, 5, 1, 0, 24), (1, 7, 1, 0, 24), (0, 3, 1, 0, 8), (1, 3, 1, 8, 16),
        (0, 4, 1, 0, 24), (1, 6, 1, 0, 24),
        (0, 1, 1, 0, 24), (1, 2, 1, 0, 24),
        (0, 0, 1, 0, 24),
    ),
)
GROUPS = (((0, 1), (2, 3, 4, 5), (6, 7)), ((0, 1, 2, 3), (4, 5), (6, 7), (8,)))


def dot(a, b, ca, cb):
    return lax.dot_general(a, b, (((ca,), (cb,)), ((), ())), preferred_element_type=F32)


def identity(n):
    rows = lax.broadcasted_iota(jnp.int32, (n, n), 0)
    return (rows == lax.broadcasted_iota(jnp.int32, (n, n), 1)).astype(BF16)


def kernel(
    tok, gw, uw, dw, cot,
    out, gt, gg, gu, gd,
    acts, weights, rows_in, X, W, WE, WP, sent, got, part, final, H,
    S, SR, T, RX, U, RY, RD, acc, gsend, ggot, grads, rows_out, results,
    in_s, out_s, w_s, w_r, di_s, di_r, ag_s, ag_r, fw_s, fw_r, rs_s, rs_r, ga_s, ga_r, sx_s, sx_r, xy_s, xy_r, gr_s, gr_r, ld_s, ld_r,
):
    row, col = lax.axis_index("row"), lax.axis_index("col")
    z, k = row // 2, row % 2
    x, y = col // 4, col % 4
    other = 1 - k
    width = gw.shape[0]
    sibling = (z * 2 + other, col)
    right = (lax.rem(z + 1, 8) * 2 + k, col)
    left = (lax.rem(z + 7, 8) * 2 + k, col)
    xpeers = {i: (row, lax.rem(x + i, 4) * 4 + y) for i in (1, 2, 3)}
    ypeers = {i: (row, x * 4 + lax.rem(y + i, 4)) for i in (1, 2, 3)}
    peers = (xpeers, ypeers)
    plane = [(row, lax.rem(x + i, 4) * 4 + lax.rem(y + j, 4)) for i in range(4) for j in range(4)][1:]

    def copy(src, dst, s, r, device):
        return pltpu.make_async_remote_copy(
            src_ref=src, dst_ref=dst, send_sem=s, recv_sem=r, device_id=device, device_id_type=MESH
        )

    started = {}

    def start(key, c):
        c.start()
        started[key] = c

    def arrive(*key):
        started[key].wait_recv()

    sent_off = []

    def settle(but=0):
        for key in list(started)[: len(started) - but]:
            if key not in sent_off:
                started[key].wait_send()
                sent_off.append(key)

    barrier = pltpu.get_barrier_semaphore()
    for device in [sibling, right, left, *plane]:
        pl.semaphore_signal(barrier, inc=1, device_id=device, device_id_type=MESH)

    first_half = lax.broadcasted_iota(jnp.int32, (PIECE, LANES), 1) < TAIL
    loads = [
        pltpu.make_async_copy(src, dst, in_s.at[i])
        for i, (src, dst) in enumerate(
            ((tok, acts.at[0]), (cot, acts.at[1]), (gw, weights.at[0]), (uw, weights.at[1]), (dw, weights.at[2]))
        )
    ]
    for c in loads:
        c.start()

    def pieces(a):
        loads[a].wait()
        one = identity(HALF)
        tails = acts[a, pl.ds(LANES, TAIL), :]
        rows_in[a, 0] = dot(one, acts[a, pl.ds(0, LANES), :], 1, 1)
        rows_in[a, 1] = dot(one, jnp.concatenate([tails, tails], axis=0), 1, 1)
        for q in range(4):
            at = [pl.ds(pl.multiple_of(lax.rem(z + ORDER[2 * q + e], 8) * PIECE, PIECE), PIECE) for e in range(2)]
            for e in range(2):
                X[a, k, q, x, y, pl.ds(e * PIECE, PIECE), :] = rows_in[a, 0, at[e], :].astype(BF16)
            X[a, k, q, x, y, pl.ds(2 * PIECE, PIECE), :] = jnp.where(
                first_half, rows_in[a, 1, at[0], :], rows_in[a, 1, at[1], :]
            ).astype(BF16)

    def direct1(a, q):
        ref = X.at[a, k, q, x, y]
        for i, device in enumerate(plane):
            start(("direct", a, q, i), copy(ref, ref, di_s.at[i], di_r.at[i], device))

    def direct2(a, q):
        for i in range(15):
            arrive("direct", a, q, i)
        to_sibling(a, q)

    def gather1(a, q):
        ref = X.at[a, k, q, x, y]
        for i in (1, 2, 3):
            start(
                ("gather", a, q, 0, i),
                copy(ref, ref, ag_s.at[a, q, 0, i - 1], ag_r.at[a, q, 0, i - 1], peers[q % 2][i]),
            )

    def gather2(a, q):
        for i in (1, 2, 3):
            arrive("gather", a, q, 0, i)
        ref = X.at[a, k, q, :, y] if q % 2 == 0 else X.at[a, k, q, x, :]
        for i in (1, 2, 3):
            start(
                ("gather", a, q, 1, i),
                copy(ref, ref, ag_s.at[a, q, 1, i - 1], ag_r.at[a, q, 1, i - 1], peers[1 - q % 2][i]),
            )

    def gather3(a, q):
        for i in (1, 2, 3):
            arrive("gather", a, q, 1, i)
        to_sibling(a, q)

    def to_sibling(a, q):
        ref = X.at[a, k, q]
        start(("pair", a, q), copy(ref, ref, fw_s.at[a, q], fw_r.at[a, q], sibling))

    def gather4(a, q):
        arrive("pair", a, q)

    mine = pl.ds(pl.multiple_of(k * BLOCK, BLOCK), BLOCK)
    theirs = pl.ds(pl.multiple_of(other * BLOCK, BLOCK), BLOCK)

    def swap_weights():
        for i in range(3):
            loads[2 + i].wait()
            start(("weight", i), copy(weights.at[i, :, theirs], W.at[i, k], w_s.at[i], w_r.at[i], sibling))
        for i in range(3):
            W[i, k] = weights[i, :, mine]
            expand(i, k)

    def expand(i, h):
        main, tail = W[i, h, pl.ds(0, LANES), :], W[i, h, pl.ds(LANES, TAIL), :]
        none = jnp.zeros_like(tail)
        for e in range(2):
            WE[e, i, h, pl.ds(0, LANES), :] = main
            WE[e, i, h, pl.ds(LANES + e * TAIL, TAIL), :] = tail
            WE[e, i, h, pl.ds(LANES + (1 - e) * TAIL, TAIL), :] = none
        WP[i, h, pl.ds(0, LANES), :] = main
        for e in range(2):
            WP[i, h, pl.ds(LANES + e * TAIL, TAIL), :] = tail

    def expand_theirs():
        for i in range(3):
            arrive("weight", i)
            expand(i, other)

    def packed(a, h, q, e, first, rows):
        span = pl.ds(first, rows // 64)
        main = X[a, h, q, span, :, pl.ds(e * PIECE, PIECE), :].reshape(rows, LANES)
        tail = X[a, h, q, span, :, pl.ds(2 * PIECE, PIECE), :].reshape(rows, LANES)
        return jnp.concatenate([main, tail], axis=1)

    def local(a, o, first, rows):
        total = None
        for h in range(2):
            p = dot(packed(a // 2, h, o // 2, o % 2, first, rows), WE[o % 2, a, h], 1, 0)
            total = p if total is None else total + p
        return total

    def half(dr):
        return pl.ds(HALF * dr, HALF)

    def chain(a, dr, s, rows):
        start(
            ("chain", a, dr, s),
            copy(
                sent.at[a, dr, s, rows],
                got.at[a, dr, s, rows],
                rs_s.at[a, dr, s],
                rs_r.at[a, dr, s],
                (right, left)[dr],
            ),
        )

    def step0(a):
        for dr in range(2):
            sent[a, dr, 0, half(dr), :] = local(a, PLACE[4], 2 * dr, HALF).astype(BF16)
            chain(a, dr, 0, half(dr))

    def step(a, s):
        for dr in range(2):
            part[dr] = local(a, PLACE[(4 - s, 4 + s)[dr]], 0, BLOCK)
        for dr in range(2):
            arrive("chain", a, dr, s - 1)
            if s == 1:
                sent[a, dr, s, half(dr), :] = (part[dr, half(dr), :] + got[a, dr, 0, half(dr), :].astype(F32)).astype(BF16)
                sent[a, dr, s, half(1 - dr), :] = part[dr, half(1 - dr), :].astype(BF16)
            else:
                sent[a, dr, s] = (part[dr] + got[a, dr, s - 1].astype(F32)).astype(BF16)
            chain(a, dr, s, pl.ds(0, BLOCK))

    def finish(a):
        final[a] = local(a, PLACE[0], 0, BLOCK)
        for dr in range(2):
            arrive("chain", a, dr, 3)
        final[a] += got[a, 0, 3].astype(F32) + got[a, 1, 3].astype(F32)

    def relay_step(m, s):
        for dr in range(2):
            places = (RIGHTWARD, LEFTWARD)[dr]
            rows = half(dr) if s == 3 else pl.ds(0, BLOCK)
            if s > 0:
                arrive("relay", m, dr, s - 1)
            start(
                ("relay", m, dr, s),
                copy(
                    H.at[m, places[s], rows],
                    H.at[m, places[s + 1], rows],
                    ga_s.at[m, dr, s],
                    ga_r.at[m, dr, s],
                    (right, left)[dr],
                ),
            )

    def relay_end(m):
        for dr in range(2):
            arrive("relay", m, dr, 3)

    def activate():
        gate, up = final[0], final[1]
        H[0, PLACE[0]] = ((gate * jax.nn.sigmoid(gate)) * up).astype(BF16)

    def activate_back():
        gate, up, gh = final[0], final[1], final[2]
        sigma = jax.nn.sigmoid(gate)
        H[1, PLACE[0]] = (gh * up * sigma * (1.0 + gate * (1.0 - sigma))).astype(BF16)
        H[2, PLACE[0]] = (gh * (gate * sigma)).astype(BF16)

    def product(i, lo, n):
        def body(o, carry):
            for h in range(2):
                if i == 0:
                    p = dot(H[0, o], WP[2, h], 1, 1)
                else:
                    p = dot(H[1, o], WP[0, h], 1, 1) + dot(H[2, o], WP[1, h], 1, 1)
                S[i, h, o, :, :, pl.ds(0, PIECE), :] = p[:, :LANES].reshape(4, 4, PIECE, LANES)
                tail = p[:, LANES:].reshape(4, 4, PIECE, LANES)
                low = lax.broadcasted_iota(jnp.int32, (4, 4, 8, LANES), 3) < TAIL
                S[i, h, o, :, :, pl.ds(PIECE, 8), :] = jnp.where(low, tail[:, :, :8], tail[:, :, 8:])
            return carry

        if n == 1:
            body(lo, 0)
        else:
            lax.fori_loop(lo, lo + n, body, 0)

    def part_of(i, u):
        cls, lo, n, r, m = PARTS[i][u]
        return cls, lo, n, pl.ds(lo, n), pl.ds(r, m)

    def products(i, g):
        for lo, n in dict.fromkeys(PARTS[i][u][1:3] for u in GROUPS[i][g]):
            product(i, lo, n)
            for u in GROUPS[i][g]:
                if PARTS[i][u][1] == lo:
                    cls, lo, n, span, rows = part_of(i, u)
                    start(
                        ("cores", i, u),
                        copy(
                            S.at[i, other, span, :, :, rows],
                            SR.at[i, span, :, :, rows],
                            sx_s.at[i, u],
                            sx_r.at[i, u],
                            sibling,
                        ),
                    )

    def scatter1(i, g):
        for u in GROUPS[i][g]:
            cls, lo, n, span, rows = part_of(i, u)
            arrive("cores", i, u)
            T[i, span, :, :, rows] = S[i, k, span, :, :, rows] + SR[i, span, :, :, rows]
            for q in (1, 2, 3):
                if cls == 0:
                    src = T.at[i, span, lax.rem(x + q, 4), :, rows]
                else:
                    src = T.at[i, span, :, lax.rem(y + q, 4), rows]
                start(
                    ("scatter", i, u, 0, q),
                    copy(
                        src,
                        RX.at[i, q - 1, span, :, rows],
                        xy_s.at[i, u, 0, q - 1],
                        xy_r.at[i, u, 0, q - 1],
                        peers[cls][q],
                    ),
                )

    def scatter2(i, g):
        for u in GROUPS[i][g]:
            cls, lo, n, span, rows = part_of(i, u)
            total = T[i, span, x, :, rows] if cls == 0 else T[i, span, :, y, rows]
            for q in (1, 2, 3):
                arrive("scatter", i, u, 0, q)
                total = total + RX[i, q - 1, span, :, rows]
            U[i, span, :, rows] = total
            for q in (1, 2, 3):
                at = lax.rem(y + q, 4) if cls == 0 else lax.rem(x + q, 4)
                start(
                    ("scatter", i, u, 1, q),
                    copy(
                        U.at[i, span, at, rows],
                        RY.at[i, q - 1, span, rows],
                        xy_s.at[i, u, 1, q - 1],
                        xy_r.at[i, u, 1, q - 1],
                        peers[1 - cls][q],
                    ),
                )

    def scatter3(i, g):
        for u in GROUPS[i][g]:
            cls, lo, n, span, rows = part_of(i, u)
            total = U[i, span, y if cls == 0 else x, rows]
            for q in (1, 2, 3):
                arrive("scatter", i, u, 1, q)
                total = total + RY[i, q - 1, span, rows]
            for p in range(n):
                rows_out[i, lax.rem(z + ORDER[lo + p], 8), rows, :] = total[p]

    def last1(i, u):
        arrive("cores", i, u)
        T[i, 0] = S[i, k, 0] + SR[i, 0]
        for n, (_, at) in enumerate(plane):
            start(
                ("last", n),
                copy(T.at[i, 0, at // 4, at % 4], RD.at[n], ld_s.at[n], ld_r.at[n], plane[n]),
            )

    def last2(i):
        total = T[i, 0, x, y]
        for n in range(15):
            arrive("last", n)
            total = total + RD[n]
        rows_out[i, lax.rem(z + ORDER[0], 8)] = total

    stores = []

    def store(src, dst):
        c = pltpu.make_async_copy(src, dst, out_s.at[len(stores)])
        c.start()
        stores.append(c)

    def deliver(i):
        one = identity(LANES)
        main = rows_out[i, :, pl.ds(0, PIECE), :].reshape(HALF, LANES)
        tail = rows_out[i, :, pl.ds(PIECE, 8), :]
        tail = jnp.concatenate([tail, tail], axis=1).reshape(HALF, LANES)
        results[i, pl.ds(0, LANES), :] = dot(one, main.astype(BF16), 1, 1).astype(BF16)
        tail = dot(one, tail.astype(BF16), 1, 1)
        low = lax.broadcasted_iota(jnp.int32, (TAIL, HALF), 1) % PIECE < 8
        results[i, pl.ds(LANES, TAIL), :] = jnp.where(low, tail[:TAIL], tail[TAIL:]).astype(BF16)
        store(results.at[i], (out, gt)[i])

    def grad(n, lo, hi):
        a, b = ((0, 1), (0, 2), (1, 0))[n]

        def body(q, carry):
            for h in range(2):
                for e in range(2):
                    p = dot(packed(a, h, q, e, 0, BLOCK), H[b, 2 * q + e], 0, 0)
                    acc[n, h, pl.ds(0, LANES), :] += p[:LANES]
                    acc[n, h, pl.ds(LANES, TAIL), :] += p[LANES + e * TAIL : LANES + (e + 1) * TAIL]
            return carry

        if hi - lo == 1:
            body(lo, 0)
        else:
            lax.fori_loop(lo, hi, body, 0)

    def grad_swap(n):
        gsend[n] = acc[n, other].astype(BF16)
        start(("grad", n), copy(gsend.at[n], ggot.at[n], gr_s.at[n], gr_r.at[n], sibling))
        grads[n, :, mine] = acc[n, k].astype(BF16)

    def grad_end(n):
        arrive("grad", n)
        grads[n, :, theirs] = ggot[n]
        store(grads.at[n], (gg, gu, gd)[n])

    pieces(0)
    pl.semaphore_wait(barrier, 18)
    direct1(0, 0)
    gather1(0, 1)
    swap_weights()
    pieces(1)
    gather1(1, 0)
    gather1(1, 1)
    gather2(0, 1)
    expand_theirs()
    direct2(0, 0)
    acc[...] = jnp.zeros_like(acc)
    gather2(1, 0)
    gather2(1, 1)
    gather1(0, 2)
    gather1(0, 3)
    gather4(0, 0)
    step0(0)
    step0(1)
    gather3(0, 1)
    gather3(1, 0)
    gather2(0, 2)
    gather2(0, 3)
    gather1(1, 2)
    gather1(1, 3)
    gather4(0, 1)
    step(0, 1)
    step(1, 1)
    gather4(1, 0)
    step0(2)
    gather3(1, 1)
    gather3(0, 2)
    gather3(0, 3)
    gather2(1, 2)
    gather2(1, 3)
    gather4(0, 2)
    gather4(0, 3)
    step(0, 2)
    step(1, 2)
    gather4(1, 1)
    step(2, 1)
    gather3(1, 2)
    gather3(1, 3)
    step(0, 3)
    step(1, 3)
    gather4(1, 2)
    gather4(1, 3)
    step(2, 2)
    finish(0)
    finish(1)
    activate()
    relay_step(0, 0)
    step(2, 3)
    relay_step(0, 1)
    finish(2)
    activate_back()
    relay_step(1, 0)
    relay_step(2, 0)
    relay_step(0, 2)
    products(0, 0)
    relay_step(1, 1)
    scatter1(0, 0)
    relay_step(2, 1)
    products(1, 0)
    grad(2, 2, 4)
    relay_step(0, 3)
    products(0, 1)
    scatter1(1, 0)
    scatter2(0, 0)
    relay_step(1, 2)
    scatter1(0, 1)
    relay_step(2, 2)
    products(1, 1)
    scatter2(1, 0)
    relay_end(0)
    products(0, 2)
    scatter1(1, 1)
    grad(2, 0, 2)
    grad_swap(2)
    scatter1(0, 2)
    relay_step(1, 3)
    scatter2(0, 1)
    relay_step(2, 3)
    settle(24)
    products(1, 2)
    scatter2(1, 1)
    scatter2(0, 2)
    scatter1(1, 2)
    relay_end(1)
    relay_end(2)
    products(1, 3)
    grad(0, 0, 4)
    grad_swap(0)
    last1(1, 8)
    scatter2(1, 2)
    grad(1, 0, 4)
    grad_swap(1)
    scatter3(0, 0)
    scatter3(0, 1)
    scatter3(0, 2)
    deliver(0)
    grad_end(2)
    scatter3(1, 0)
    scatter3(1, 1)
    grad_end(0)
    grad_end(1)
    settle(18)
    scatter3(1, 2)
    last2(1)
    deliver(1)
    for c in stores:
        c.wait()
    settle()


def hand_over(*refs):
    held, results, kept, sems = refs[:5], refs[5:10], refs[10:15], refs[15]
    loads = [pltpu.make_async_copy(held[i], kept[i], sems.at[0, i]) for i in range(5)]
    stores = [pltpu.make_async_copy(kept[i], results[i], sems.at[1, i]) for i in range(5)]
    for c in loads:
        c.start()
    for load, store in zip(loads, stores):
        load.wait()
        store.start()
    for c in stores:
        c.wait()


def body(tokens, gate_weight, up_weight, down_weight, cotangent):
    n_tok, width = tokens.shape
    hidden = gate_weight.shape[1]
    dma = pltpu.SemaphoreType.DMA
    V = pltpu.VMEM
    act = jax.ShapeDtypeStruct((width, n_tok), BF16)
    weight = jax.ShapeDtypeStruct((width, hidden), BF16)
    shapes = (act, act, weight, weight, weight)
    scratch = [
        V((2, width, n_tok), BF16),
        V((3, width, hidden), BF16),
        V((2, 2, n_tok, LANES), F32),
        V((2, 2, 4, 4, 4, 3 * PIECE, LANES), BF16),
        V((3, 2, width, BLOCK), BF16),
        V((2, 3, 2, 2 * LANES, BLOCK), BF16),
        V((3, 2, 2 * LANES, BLOCK), BF16),
        V((3, 2, 4, BLOCK, BLOCK), BF16),
        V((3, 2, 4, BLOCK, BLOCK), BF16),
        V((2, BLOCK, BLOCK), F32),
        V((3, BLOCK, BLOCK), F32),
        V((3, 8, BLOCK, BLOCK), BF16),
        V((2, 2, 8, 4, 4, 24, LANES), F32),
        V((2, 8, 4, 4, 24, LANES), F32),
        V((2, 8, 4, 4, 24, LANES), F32),
        V((2, 3, 8, 4, 24, LANES), F32),
        V((2, 8, 4, 24, LANES), F32),
        V((2, 3, 8, 24, LANES), F32),
        V((15, 24, LANES), F32),
        V((3, 2, width, BLOCK), F32),
        V((3, width, BLOCK), BF16),
        V((3, width, BLOCK), BF16),
        V((3, width, hidden), BF16),
        V((2, 8, 24, LANES), F32),
        V((2, width, n_tok), BF16),
        dma((5,)), dma((5,)),
        dma((3,)), dma((3,)),
        dma((15,)), dma((15,)),
        dma((2, 4, 2, 3)), dma((2, 4, 2, 3)),
        dma((2, 4)), dma((2, 4)),
        dma((3, 2, 4)), dma((3, 2, 4)),
        dma((3, 2, 4)), dma((3, 2, 4)),
        dma((2, 10)), dma((2, 10)),
        dma((2, 10, 2, 3)), dma((2, 10, 2, 3)),
        dma((3,)), dma((3,)),
        dma((15,)), dma((15,)),
    ]
    anywhere = pl.BlockSpec(memory_space=pl.ANY)
    held = pl.pallas_call(
        kernel,
        out_shape=shapes,
        in_specs=[anywhere] * 5,
        out_specs=(anywhere,) * 5,
        scratch_shapes=scratch,
        name="feed_forward",
        compiler_params=pltpu.CompilerParams(
            collective_id=0, has_side_effects=True, vmem_limit_bytes=56 * 2**20
        ),
    )(tokens.T, gate_weight, up_weight, down_weight.T, cotangent.T)
    results = pl.pallas_call(
        hand_over,
        out_shape=shapes,
        in_specs=[anywhere] * 5,
        out_specs=(anywhere,) * 5,
        scratch_shapes=[V(v.shape, BF16) for v in shapes] + [dma((2, 5))],
        name="hand_over",
        compiler_params=pltpu.CompilerParams(vmem_limit_bytes=60 * 2**20),
    )(*held)
    return results[0].T, results[1].T, results[2], results[3], results[4].T


def solution(mesh):
    return jax.shard_map(
        body,
        mesh=mesh,
        in_specs=(
            P("col", "row"),
            P("row", "col"),
            P("row", "col"),
            P("col", "row"),
            P("col", "row"),
        ),
        out_specs=(
            P("col", "row"),
            P("col", "row"),
            P("row", "col"),
            P("row", "col"),
            P("col", "row"),
        ),
        check_vma=False,
    )
```

```python
import jax
import jax.numpy as jnp
from jax import lax
from jax.experimental import pallas as pl
from jax.experimental.pallas import tpu as pltpu
from jax.sharding import PartitionSpec as P

MESH = pl.DeviceIdType.MESH
F32 = jnp.float32
BF16 = jnp.bfloat16

ORDER = (4, 3, 5, 0, 2, 1, 6, 7)
PLACE = {d: o for o, d in enumerate(ORDER)}
PIECE = 16
LANES = 128
TAIL = 64
BLOCK = 256
HALF = 128
RIGHTWARD = tuple(PLACE[d] for d in (0, 7, 6, 5, 4))
LEFTWARD = tuple(PLACE[d] for d in (0, 1, 2, 3, 4))
PARTS = (
    (
        (0, 4, 2, 0, 24), (1, 6, 2, 0, 24),
        (0, 1, 1, 0, 24), (1, 2, 1, 0, 24), (0, 3, 1, 0, 16), (1, 3, 1, 16, 8),
        (0, 0, 1, 0, 8), (1, 0, 1, 8, 16),
    ),
    (
        (0, 5, 1, 0, 24), (1, 7, 1, 0, 24), (0, 3, 1, 0, 8), (1, 3, 1, 8, 16),
        (0, 4, 1, 0, 24), (1, 6, 1, 0, 24),
        (0, 1, 1, 0, 24), (1, 2, 1, 0, 24),
        (0, 0, 1, 0, 24),
    ),
)
GROUPS = (((0, 1), (2, 3, 4, 5), (6, 7)), ((0, 1, 2, 3), (4, 5), (6, 7), (8,)))


def dot(a, b, ca, cb):
    return lax.dot_general(a, b, (((ca,), (cb,)), ((), ())), preferred_element_type=F32)


def identity(n):
    rows = lax.broadcasted_iota(jnp.int32, (n, n), 0)
    return (rows == lax.broadcasted_iota(jnp.int32, (n, n), 1)).astype(BF16)


def kernel(
    tok, gw, uw, dw, cot,
    out, gt, gg, gu, gd,
    acts, weights, rows_in, X, W, WE, WP, sent, got, part, final, H,
    S, SR, T, RX, U, RY, RD, acc, gsend, ggot, grads, rows_out, results,
    in_s, out_s, w_s, w_r, di_s, di_r, ag_s, ag_r, fw_s, fw_r, rs_s, rs_r, ga_s, ga_r, sx_s, sx_r, xy_s, xy_r, gr_s, gr_r, ld_s, ld_r,
):
    row, col = lax.axis_index("row"), lax.axis_index("col")
    z, k = row // 2, row % 2
    x, y = col // 4, col % 4
    other = 1 - k
    width = gw.shape[0]
    sibling = (z * 2 + other, col)
    right = (lax.rem(z + 1, 8) * 2 + k, col)
    left = (lax.rem(z + 7, 8) * 2 + k, col)
    xpeers = {i: (row, lax.rem(x + i, 4) * 4 + y) for i in (1, 2, 3)}
    ypeers = {i: (row, x * 4 + lax.rem(y + i, 4)) for i in (1, 2, 3)}
    peers = (xpeers, ypeers)
    plane = [(row, lax.rem(x + i, 4) * 4 + lax.rem(y + j, 4)) for i in range(4) for j in range(4)][1:]

    def copy(src, dst, s, r, device):
        return pltpu.make_async_remote_copy(
            src_ref=src, dst_ref=dst, send_sem=s, recv_sem=r, device_id=device, device_id_type=MESH
        )

    started = {}

    def start(key, c):
        c.start()
        started[key] = c

    def arrive(*key):
        started[key].wait_recv()

    sent_off = []

    def settle(but=0):
        for key in list(started)[: len(started) - but]:
            if key not in sent_off:
                started[key].wait_send()
                sent_off.append(key)

    barrier = pltpu.get_barrier_semaphore()
    for device in [sibling, right, left, *plane]:
        pl.semaphore_signal(barrier, inc=1, device_id=device, device_id_type=MESH)

    first_half = lax.broadcasted_iota(jnp.int32, (PIECE, LANES), 1) < TAIL
    loads = [
        pltpu.make_async_copy(src, dst, in_s.at[i])
        for i, (src, dst) in enumerate(
            ((tok, acts.at[0]), (cot, acts.at[1]), (gw, weights.at[0]), (uw, weights.at[1]), (dw, weights.at[2]))
        )
    ]
    for c in loads:
        c.start()

    def pieces(a):
        loads[a].wait()
        one = identity(HALF)
        tails = acts[a, pl.ds(LANES, TAIL), :]
        rows_in[a, 0] = dot(one, acts[a, pl.ds(0, LANES), :], 1, 1)
        rows_in[a, 1] = dot(one, jnp.concatenate([tails, tails], axis=0), 1, 1)
        for q in range(4):
            at = [pl.ds(pl.multiple_of(lax.rem(z + ORDER[2 * q + e], 8) * PIECE, PIECE), PIECE) for e in range(2)]
            for e in range(2):
                X[a, k, q, x, y, pl.ds(e * PIECE, PIECE), :] = rows_in[a, 0, at[e], :].astype(BF16)
            X[a, k, q, x, y, pl.ds(2 * PIECE, PIECE), :] = jnp.where(
                first_half, rows_in[a, 1, at[0], :], rows_in[a, 1, at[1], :]
            ).astype(BF16)

    def direct1(a, q):
        ref = X.at[a, k, q, x, y]
        for i, device in enumerate(plane):
            start(("direct", a, q, i), copy(ref, ref, di_s.at[i], di_r.at[i], device))

    def direct2(a, q):
        for i in range(15):
            arrive("direct", a, q, i)
        to_sibling(a, q)

    def gather1(a, q):
        ref = X.at[a, k, q, x, y]
        for i in (1, 2, 3):
            start(
                ("gather", a, q, 0, i),
                copy(ref, ref, ag_s.at[a, q, 0, i - 1], ag_r.at[a, q, 0, i - 1], peers[q % 2][i]),
            )

    def gather2(a, q):
        for i in (1, 2, 3):
            arrive("gather", a, q, 0, i)
        ref = X.at[a, k, q, :, y] if q % 2 == 0 else X.at[a, k, q, x, :]
        for i in (1, 2, 3):
            start(
                ("gather", a, q, 1, i),
                copy(ref, ref, ag_s.at[a, q, 1, i - 1], ag_r.at[a, q, 1, i - 1], peers[1 - q % 2][i]),
            )

    def gather3(a, q):
        for i in (1, 2, 3):
            arrive("gather", a, q, 1, i)
        to_sibling(a, q)

    def to_sibling(a, q):
        ref = X.at[a, k, q]
        start(("pair", a, q), copy(ref, ref, fw_s.at[a, q], fw_r.at[a, q], sibling))

    def gather4(a, q):
        arrive("pair", a, q)

    mine = pl.ds(pl.multiple_of(k * BLOCK, BLOCK), BLOCK)
    theirs = pl.ds(pl.multiple_of(other * BLOCK, BLOCK), BLOCK)

    def swap_weights():
        for i in range(3):
            loads[2 + i].wait()
            start(("weight", i), copy(weights.at[i, :, theirs], W.at[i, k], w_s.at[i], w_r.at[i], sibling))
        for i in range(3):
            W[i, k] = weights[i, :, mine]
            expand(i, k)

    def expand(i, h):
        main, tail = W[i, h, pl.ds(0, LANES), :], W[i, h, pl.ds(LANES, TAIL), :]
        none = jnp.zeros_like(tail)
        for e in range(2):
            WE[e, i, h, pl.ds(0, LANES), :] = main
            WE[e, i, h, pl.ds(LANES + e * TAIL, TAIL), :] = tail
            WE[e, i, h, pl.ds(LANES + (1 - e) * TAIL, TAIL), :] = none
        WP[i, h, pl.ds(0, LANES), :] = main
        for e in range(2):
            WP[i, h, pl.ds(LANES + e * TAIL, TAIL), :] = tail

    def expand_theirs():
        for i in range(3):
            arrive("weight", i)
            expand(i, other)

    def packed(a, h, q, e, first, rows):
        span = pl.ds(first, rows // 64)
        main = X[a, h, q, span, :, pl.ds(e * PIECE, PIECE), :].reshape(rows, LANES)
        tail = X[a, h, q, span, :, pl.ds(2 * PIECE, PIECE), :].reshape(rows, LANES)
        return jnp.concatenate([main, tail], axis=1)

    def local(a, o, first, rows):
        total = None
        for h in range(2):
            p = dot(packed(a // 2, h, o // 2, o % 2, first, rows), WE[o % 2, a, h], 1, 0)
            total = p if total is None else total + p
        return total

    def half(dr):
        return pl.ds(HALF * dr, HALF)

    def chain(a, dr, s, rows):
        start(
            ("chain", a, dr, s),
            copy(
                sent.at[a, dr, s, rows],
                got.at[a, dr, s, rows],
                rs_s.at[a, dr, s],
                rs_r.at[a, dr, s],
                (right, left)[dr],
            ),
        )

    def step0(a):
        for dr in range(2):
            sent[a, dr, 0, half(dr), :] = local(a, PLACE[4], 2 * dr, HALF).astype(BF16)
            chain(a, dr, 0, half(dr))

    def step(a, s):
        for dr in range(2):
            part[dr] = local(a, PLACE[(4 - s, 4 + s)[dr]], 0, BLOCK)
        for dr in range(2):
            arrive("chain", a, dr, s - 1)
            if s == 1:
                sent[a, dr, s, half(dr), :] = (part[dr, half(dr), :] + got[a, dr, 0, half(dr), :].astype(F32)).astype(BF16)
                sent[a, dr, s, half(1 - dr), :] = part[dr, half(1 - dr), :].astype(BF16)
            else:
                sent[a, dr, s] = (part[dr] + got[a, dr, s - 1].astype(F32)).astype(BF16)
            chain(a, dr, s, pl.ds(0, BLOCK))

    def finish(a):
        final[a] = local(a, PLACE[0], 0, BLOCK)
        for dr in range(2):
            arrive("chain", a, dr, 3)
        final[a] += got[a, 0, 3].astype(F32) + got[a, 1, 3].astype(F32)

    def relay_step(m, s):
        for dr in range(2):
            places = (RIGHTWARD, LEFTWARD)[dr]
            rows = half(dr) if s == 3 else pl.ds(0, BLOCK)
            if s > 0:
                arrive("relay", m, dr, s - 1)
            start(
                ("relay", m, dr, s),
                copy(
                    H.at[m, places[s], rows],
                    H.at[m, places[s + 1], rows],
                    ga_s.at[m, dr, s],
                    ga_r.at[m, dr, s],
                    (right, left)[dr],
                ),
            )

    def relay_end(m):
        for dr in range(2):
            arrive("relay", m, dr, 3)

    def activate():
        gate, up = final[0], final[1]
        H[0, PLACE[0]] = ((gate * jax.nn.sigmoid(gate)) * up).astype(BF16)

    def activate_back():
        gate, up, gh = final[0], final[1], final[2]
        sigma = jax.nn.sigmoid(gate)
        H[1, PLACE[0]] = (gh * up * sigma * (1.0 + gate * (1.0 - sigma))).astype(BF16)
        H[2, PLACE[0]] = (gh * (gate * sigma)).astype(BF16)

    def product(i, lo, n):
        def body(o, carry):
            for h in range(2):
                if i == 0:
                    p = dot(H[0, o], WP[2, h], 1, 1)
                else:
                    p = dot(H[1, o], WP[0, h], 1, 1) + dot(H[2, o], WP[1, h], 1, 1)
                S[i, h, o, :, :, pl.ds(0, PIECE), :] = p[:, :LANES].reshape(4, 4, PIECE, LANES)
                tail = p[:, LANES:].reshape(4, 4, PIECE, LANES)
                low = lax.broadcasted_iota(jnp.int32, (4, 4, 8, LANES), 3) < TAIL
                S[i, h, o, :, :, pl.ds(PIECE, 8), :] = jnp.where(low, tail[:, :, :8], tail[:, :, 8:])
            return carry

        if n == 1:
            body(lo, 0)
        else:
            lax.fori_loop(lo, lo + n, body, 0)

    def part_of(i, u):
        cls, lo, n, r, m = PARTS[i][u]
        return cls, lo, n, pl.ds(lo, n), pl.ds(r, m)

    def products(i, g):
        for lo, n in dict.fromkeys(PARTS[i][u][1:3] for u in GROUPS[i][g]):
            product(i, lo, n)
            for u in GROUPS[i][g]:
                if PARTS[i][u][1] == lo:
                    cls, lo, n, span, rows = part_of(i, u)
                    start(
                        ("cores", i, u),
                        copy(
                            S.at[i, other, span, :, :, rows],
                            SR.at[i, span, :, :, rows],
                            sx_s.at[i, u],
                            sx_r.at[i, u],
                            sibling,
                        ),
                    )

    def scatter1(i, g):
        for u in GROUPS[i][g]:
            cls, lo, n, span, rows = part_of(i, u)
            arrive("cores", i, u)
            T[i, span, :, :, rows] = S[i, k, span, :, :, rows] + SR[i, span, :, :, rows]
            for q in (1, 2, 3):
                if cls == 0:
                    src = T.at[i, span, lax.rem(x + q, 4), :, rows]
                else:
                    src = T.at[i, span, :, lax.rem(y + q, 4), rows]
                start(
                    ("scatter", i, u, 0, q),
                    copy(
                        src,
                        RX.at[i, q - 1, span, :, rows],
                        xy_s.at[i, u, 0, q - 1],
                        xy_r.at[i, u, 0, q - 1],
                        peers[cls][q],
                    ),
                )

    def scatter2(i, g):
        for u in GROUPS[i][g]:
            cls, lo, n, span, rows = part_of(i, u)
            total = T[i, span, x, :, rows] if cls == 0 else T[i, span, :, y, rows]
            for q in (1, 2, 3):
                arrive("scatter", i, u, 0, q)
                total = total + RX[i, q - 1, span, :, rows]
            U[i, span, :, rows] = total
            for q in (1, 2, 3):
                at = lax.rem(y + q, 4) if cls == 0 else lax.rem(x + q, 4)
                start(
                    ("scatter", i, u, 1, q),
                    copy(
                        U.at[i, span, at, rows],
                        RY.at[i, q - 1, span, rows],
                        xy_s.at[i, u, 1, q - 1],
                        xy_r.at[i, u, 1, q - 1],
                        peers[1 - cls][q],
                    ),
                )

    def scatter3(i, g):
        for u in GROUPS[i][g]:
            cls, lo, n, span, rows = part_of(i, u)
            total = U[i, span, y if cls == 0 else x, rows]
            for q in (1, 2, 3):
                arrive("scatter", i, u, 1, q)
                total = total + RY[i, q - 1, span, rows]
            for p in range(n):
                rows_out[i, lax.rem(z + ORDER[lo + p], 8), rows, :] = total[p]

    def last1(i, u):
        arrive("cores", i, u)
        T[i, 0] = S[i, k, 0] + SR[i, 0]
        for n, (_, at) in enumerate(plane):
            start(
                ("last", n),
                copy(T.at[i, 0, at // 4, at % 4], RD.at[n], ld_s.at[n], ld_r.at[n], plane[n]),
            )

    def last2(i):
        total = T[i, 0, x, y]
        for n in range(15):
            arrive("last", n)
            total = total + RD[n]
        rows_out[i, lax.rem(z + ORDER[0], 8)] = total

    stores = []

    def store(src, dst):
        c = pltpu.make_async_copy(src, dst, out_s.at[len(stores)])
        c.start()
        stores.append(c)

    def deliver(i):
        one = identity(LANES)
        main = rows_out[i, :, pl.ds(0, PIECE), :].reshape(HALF, LANES)
        tail = rows_out[i, :, pl.ds(PIECE, 8), :]
        tail = jnp.concatenate([tail, tail], axis=1).reshape(HALF, LANES)
        results[i, pl.ds(0, LANES), :] = dot(one, main.astype(BF16), 1, 1).astype(BF16)
        tail = dot(one, tail.astype(BF16), 1, 1)
        low = lax.broadcasted_iota(jnp.int32, (TAIL, HALF), 1) % PIECE < 8
        results[i, pl.ds(LANES, TAIL), :] = jnp.where(low, tail[:TAIL], tail[TAIL:]).astype(BF16)
        store(results.at[i], (out, gt)[i])

    def grad(n, lo, hi):
        a, b = ((0, 1), (0, 2), (1, 0))[n]

        def body(q, carry):
            for h in range(2):
                for e in range(2):
                    p = dot(packed(a, h, q, e, 0, BLOCK), H[b, 2 * q + e], 0, 0)
                    acc[n, h, pl.ds(0, LANES), :] += p[:LANES]
                    acc[n, h, pl.ds(LANES, TAIL), :] += p[LANES + e * TAIL : LANES + (e + 1) * TAIL]
            return carry

        if hi - lo == 1:
            body(lo, 0)
        else:
            lax.fori_loop(lo, hi, body, 0)

    def grad_swap(n):
        gsend[n] = acc[n, other].astype(BF16)
        start(("grad", n), copy(gsend.at[n], ggot.at[n], gr_s.at[n], gr_r.at[n], sibling))
        grads[n, :, mine] = acc[n, k].astype(BF16)

    def grad_end(n):
        arrive("grad", n)
        grads[n, :, theirs] = ggot[n]
        store(grads.at[n], (gg, gu, gd)[n])

    pieces(0)
    pl.semaphore_wait(barrier, 18)
    direct1(0, 0)
    gather1(0, 1)
    gather1(0, 2)
    gather1(0, 3)
    swap_weights()
    pieces(1)
    gather1(1, 0)
    gather1(1, 1)
    gather2(0, 1)
    gather2(1, 0)
    expand_theirs()
    direct2(0, 0)
    gather2(0, 2)
    gather2(0, 3)
    gather2(1, 1)
    gather1(1, 2)
    gather1(1, 3)
    acc[...] = jnp.zeros_like(acc)
    gather3(0, 1)
    gather4(0, 0)
    step0(0)
    step0(1)
    gather3(1, 0)
    gather4(0, 1)
    step(0, 1)
    step(1, 1)
    gather3(0, 2)
    gather3(0, 3)
    gather2(1, 2)
    gather2(1, 3)
    gather4(1, 0)
    step0(2)
    gather3(1, 1)
    gather4(0, 2)
    gather4(0, 3)
    step(0, 2)
    step(1, 2)
    gather4(1, 1)
    step(2, 1)
    gather3(1, 2)
    gather3(1, 3)
    step(0, 3)
    step(1, 3)
    gather4(1, 2)
    gather4(1, 3)
    step(2, 2)
    finish(0)
    finish(1)
    activate()
    relay_step(0, 0)
    step(2, 3)
    relay_step(0, 1)
    finish(2)
    activate_back()
    relay_step(1, 0)
    relay_step(2, 0)
    relay_step(0, 2)
    products(0, 0)
    relay_step(1, 1)
    relay_step(2, 1)
    products(1, 0)
    scatter1(0, 0)
    relay_step(0, 3)
    products(0, 1)
    grad(2, 2, 4)
    relay_step(1, 2)
    scatter1(1, 0)
    relay_step(2, 2)
    scatter2(0, 0)
    products(1, 1)
    scatter1(0, 1)
    relay_end(0)
    products(0, 2)
    grad(2, 0, 2)
    grad_swap(2)
    relay_step(1, 3)
    scatter2(1, 0)
    scatter1(1, 1)
    scatter1(0, 2)
    relay_step(2, 3)
    products(1, 2)
    settle(24)
    scatter2(0, 1)
    scatter1(1, 2)
    relay_end(1)
    relay_end(2)
    products(1, 3)
    grad(0, 0, 4)
    grad_swap(0)
    last1(1, 8)
    scatter2(1, 1)
    scatter2(0, 2)
    scatter2(1, 2)
    grad(1, 0, 4)
    grad_swap(1)
    scatter3(0, 0)
    scatter3(0, 1)
    scatter3(0, 2)
    deliver(0)
    grad_end(2)
    scatter3(1, 0)
    scatter3(1, 1)
    grad_end(0)
    grad_end(1)
    settle(18)
    scatter3(1, 2)
    last2(1)
    deliver(1)
    for c in stores:
        c.wait()
    settle()


def hand_over(*refs):
    held, results, kept, sems = refs[:5], refs[5:10], refs[10:15], refs[15]
    loads = [pltpu.make_async_copy(held[i], kept[i], sems.at[0, i]) for i in range(5)]
    stores = [pltpu.make_async_copy(kept[i], results[i], sems.at[1, i]) for i in range(5)]
    for c in loads:
        c.start()
    for load, store in zip(loads, stores):
        load.wait()
        store.start()
    for c in stores:
        c.wait()


def body(tokens, gate_weight, up_weight, down_weight, cotangent):
    n_tok, width = tokens.shape
    hidden = gate_weight.shape[1]
    dma = pltpu.SemaphoreType.DMA
    V = pltpu.VMEM
    act = jax.ShapeDtypeStruct((width, n_tok), BF16)
    weight = jax.ShapeDtypeStruct((width, hidden), BF16)
    shapes = (act, act, weight, weight, weight)
    scratch = [
        V((2, width, n_tok), BF16),
        V((3, width, hidden), BF16),
        V((2, 2, n_tok, LANES), F32),
        V((2, 2, 4, 4, 4, 3 * PIECE, LANES), BF16),
        V((3, 2, width, BLOCK), BF16),
        V((2, 3, 2, 2 * LANES, BLOCK), BF16),
        V((3, 2, 2 * LANES, BLOCK), BF16),
        V((3, 2, 4, BLOCK, BLOCK), BF16),
        V((3, 2, 4, BLOCK, BLOCK), BF16),
        V((2, BLOCK, BLOCK), F32),
        V((3, BLOCK, BLOCK), F32),
        V((3, 8, BLOCK, BLOCK), BF16),
        V((2, 2, 8, 4, 4, 24, LANES), F32),
        V((2, 8, 4, 4, 24, LANES), F32),
        V((2, 8, 4, 4, 24, LANES), F32),
        V((2, 3, 8, 4, 24, LANES), F32),
        V((2, 8, 4, 24, LANES), F32),
        V((2, 3, 8, 24, LANES), F32),
        V((15, 24, LANES), F32),
        V((3, 2, width, BLOCK), F32),
        V((3, width, BLOCK), BF16),
        V((3, width, BLOCK), BF16),
        V((3, width, hidden), BF16),
        V((2, 8, 24, LANES), F32),
        V((2, width, n_tok), BF16),
        dma((5,)), dma((5,)),
        dma((3,)), dma((3,)),
        dma((15,)), dma((15,)),
        dma((2, 4, 2, 3)), dma((2, 4, 2, 3)),
        dma((2, 4)), dma((2, 4)),
        dma((3, 2, 4)), dma((3, 2, 4)),
        dma((3, 2, 4)), dma((3, 2, 4)),
        dma((2, 10)), dma((2, 10)),
        dma((2, 10, 2, 3)), dma((2, 10, 2, 3)),
        dma((3,)), dma((3,)),
        dma((15,)), dma((15,)),
    ]
    anywhere = pl.BlockSpec(memory_space=pl.ANY)
    held = pl.pallas_call(
        kernel,
        out_shape=shapes,
        in_specs=[anywhere] * 5,
        out_specs=(anywhere,) * 5,
        scratch_shapes=scratch,
        name="feed_forward",
        compiler_params=pltpu.CompilerParams(
            collective_id=0, has_side_effects=True, vmem_limit_bytes=56 * 2**20
        ),
    )(tokens.T, gate_weight, up_weight, down_weight.T, cotangent.T)
    results = pl.pallas_call(
        hand_over,
        out_shape=shapes,
        in_specs=[anywhere] * 5,
        out_specs=(anywhere,) * 5,
        scratch_shapes=[V(v.shape, BF16) for v in shapes] + [dma((2, 5))],
        name="hand_over",
        compiler_params=pltpu.CompilerParams(vmem_limit_bytes=60 * 2**20),
    )(*held)
    return results[0].T, results[1].T, results[2], results[3], results[4].T


def solution(mesh):
    return jax.shard_map(
        body,
        mesh=mesh,
        in_specs=(
            P("col", "row"),
            P("row", "col"),
            P("row", "col"),
            P("col", "row"),
            P("col", "row"),
        ),
        out_specs=(
            P("col", "row"),
            P("col", "row"),
            P("row", "col"),
            P("row", "col"),
            P("col", "row"),
        ),
        check_vma=False,
    )
```

```python
import jax
import jax.numpy as jnp
from jax import lax
from jax.experimental import pallas as pl
from jax.experimental.pallas import tpu as pltpu
from jax.sharding import PartitionSpec as P

MESH = pl.DeviceIdType.MESH
F32 = jnp.float32
BF16 = jnp.bfloat16

ORDER = (4, 3, 5, 0, 2, 1, 6, 7)
PLACE = {d: o for o, d in enumerate(ORDER)}
PIECE = 16
LANES = 128
TAIL = 64
BLOCK = 256
HALF = 128
RIGHTWARD = tuple(PLACE[d] for d in (0, 7, 6, 5, 4))
LEFTWARD = tuple(PLACE[d] for d in (0, 1, 2, 3, 4))
PARTS = (
    (
        (0, 4, 2, 0, 24), (1, 6, 2, 0, 24),
        (0, 1, 1, 0, 24), (1, 2, 1, 0, 24), (0, 3, 1, 0, 16), (1, 3, 1, 16, 8),
        (0, 0, 1, 0, 8), (1, 0, 1, 8, 16),
    ),
    (
        (0, 5, 1, 0, 24), (1, 7, 1, 0, 24), (0, 3, 1, 0, 8), (1, 3, 1, 8, 16),
        (0, 4, 1, 0, 24), (1, 6, 1, 0, 24),
        (0, 1, 1, 0, 24), (1, 2, 1, 0, 24),
        (0, 0, 1, 0, 24),
    ),
)
GROUPS = (((0, 1), (2, 3, 4, 5), (6, 7)), ((0, 1, 2, 3), (4, 5), (6, 7), (8,)))


def dot(a, b, ca, cb):
    return lax.dot_general(a, b, (((ca,), (cb,)), ((), ())), preferred_element_type=F32)


def identity(n):
    rows = lax.broadcasted_iota(jnp.int32, (n, n), 0)
    return (rows == lax.broadcasted_iota(jnp.int32, (n, n), 1)).astype(BF16)


def kernel(
    tok, gw, uw, dw, cot,
    out, gt, gg, gu, gd,
    acts, weights, rows_in, X, W, WE, WP, sent, got, part, ahead, final, H,
    S, SR, T, RX, U, RY, RD, acc, gsend, ggot, grads, rows_out, results,
    in_s, out_s, w_s, w_r, di_s, di_r, ag_s, ag_r, fw_s, fw_r, rs_s, rs_r, ga_s, ga_r, sx_s, sx_r, xy_s, xy_r, gr_s, gr_r, ld_s, ld_r,
):
    row, col = lax.axis_index("row"), lax.axis_index("col")
    z, k = row // 2, row % 2
    x, y = col // 4, col % 4
    other = 1 - k
    width = gw.shape[0]
    sibling = (z * 2 + other, col)
    right = (lax.rem(z + 1, 8) * 2 + k, col)
    left = (lax.rem(z + 7, 8) * 2 + k, col)
    xpeers = {i: (row, lax.rem(x + i, 4) * 4 + y) for i in (1, 2, 3)}
    ypeers = {i: (row, x * 4 + lax.rem(y + i, 4)) for i in (1, 2, 3)}
    peers = (xpeers, ypeers)
    hops = sorted(((i, j) for i in range(4) for j in range(4)), key=lambda v: -(min(v[0], 4 - v[0]) + min(v[1], 4 - v[1])))
    plane = [(row, lax.rem(x + i, 4) * 4 + lax.rem(y + j, 4)) for i, j in hops[:15]]

    def copy(src, dst, s, r, device):
        return pltpu.make_async_remote_copy(
            src_ref=src, dst_ref=dst, send_sem=s, recv_sem=r, device_id=device, device_id_type=MESH
        )

    started = {}

    def start(key, c):
        c.start()
        started[key] = c

    def arrive(*key):
        started[key].wait_recv()

    sent_off = []

    def settle(but=0):
        for key in list(started)[: len(started) - but]:
            if key not in sent_off:
                started[key].wait_send()
                sent_off.append(key)

    first_half = lax.broadcasted_iota(jnp.int32, (PIECE, LANES), 1) < TAIL
    loads = [
        pltpu.make_async_copy(src, dst, in_s.at[i])
        for i, (src, dst) in enumerate(
            ((tok, acts.at[0]), (cot, acts.at[1]), (gw, weights.at[0]), (uw, weights.at[1]), (dw, weights.at[2]))
        )
    ]
    for c in loads:
        c.start()

    barrier = pltpu.get_barrier_semaphore()
    for device in [sibling, right, left, *plane]:
        pl.semaphore_signal(barrier, inc=1, device_id=device, device_id_type=MESH)

    def pieces(a):
        loads[a].wait()
        one = identity(HALF)
        tails = acts[a, pl.ds(LANES, TAIL), :]
        rows_in[a, 0] = dot(one, acts[a, pl.ds(0, LANES), :], 1, 1)
        rows_in[a, 1] = dot(one, jnp.concatenate([tails, tails], axis=0), 1, 1)

    def piece(a, q):
        at = [pl.ds(pl.multiple_of(lax.rem(z + ORDER[2 * q + e], 8) * PIECE, PIECE), PIECE) for e in range(2)]
        for e in range(2):
            X[a, k, q, x, y, pl.ds(e * PIECE, PIECE), :] = rows_in[a, 0, at[e], :].astype(BF16)
        X[a, k, q, x, y, pl.ds(2 * PIECE, PIECE), :] = jnp.where(
            first_half, rows_in[a, 1, at[0], :], rows_in[a, 1, at[1], :]
        ).astype(BF16)

    def direct1(a, q):
        ref = X.at[a, k, q, x, y]
        for i, device in enumerate(plane):
            start(("direct", a, q, i), copy(ref, ref, di_s.at[i], di_r.at[i], device))

    def direct2(a, q):
        for i in range(15):
            arrive("direct", a, q, i)
        to_sibling(a, q)

    def gather1(a, q):
        ref = X.at[a, k, q, x, y]
        for i in (1, 2, 3):
            start(
                ("gather", a, q, 0, i),
                copy(ref, ref, ag_s.at[a, q, 0, i - 1], ag_r.at[a, q, 0, i - 1], peers[q % 2][i]),
            )

    def gather2(a, q):
        for i in (1, 2, 3):
            arrive("gather", a, q, 0, i)
        ref = X.at[a, k, q, :, y] if q % 2 == 0 else X.at[a, k, q, x, :]
        for i in (1, 2, 3):
            start(
                ("gather", a, q, 1, i),
                copy(ref, ref, ag_s.at[a, q, 1, i - 1], ag_r.at[a, q, 1, i - 1], peers[1 - q % 2][i]),
            )

    def gather3(a, q):
        for i in (1, 2, 3):
            arrive("gather", a, q, 1, i)
        to_sibling(a, q)

    def to_sibling(a, q):
        ref = X.at[a, k, q]
        start(("pair", a, q), copy(ref, ref, fw_s.at[a, q], fw_r.at[a, q], sibling))

    def gather4(a, q):
        arrive("pair", a, q)

    mine = pl.ds(pl.multiple_of(k * BLOCK, BLOCK), BLOCK)
    theirs = pl.ds(pl.multiple_of(other * BLOCK, BLOCK), BLOCK)

    def swap_weights():
        for i in range(3):
            loads[2 + i].wait()
            start(("weight", i), copy(weights.at[i, :, theirs], W.at[i, k], w_s.at[i], w_r.at[i], sibling))
        for i in range(3):
            W[i, k] = weights[i, :, mine]
            expand(i, k)

    def expand(i, h):
        main, tail = W[i, h, pl.ds(0, LANES), :], W[i, h, pl.ds(LANES, TAIL), :]
        none = jnp.zeros_like(tail)
        for e in range(2):
            WE[e, i, h, pl.ds(0, LANES), :] = main
            WE[e, i, h, pl.ds(LANES + e * TAIL, TAIL), :] = tail
            WE[e, i, h, pl.ds(LANES + (1 - e) * TAIL, TAIL), :] = none
        WP[i, h, pl.ds(0, LANES), :] = main
        for e in range(2):
            WP[i, h, pl.ds(LANES + e * TAIL, TAIL), :] = tail

    def expand_theirs():
        for i in range(3):
            arrive("weight", i)
            expand(i, other)

    def packed(a, h, q, e, first, rows):
        span = pl.ds(first, rows // 64)
        main = X[a, h, q, span, :, pl.ds(e * PIECE, PIECE), :].reshape(rows, LANES)
        tail = X[a, h, q, span, :, pl.ds(2 * PIECE, PIECE), :].reshape(rows, LANES)
        return jnp.concatenate([main, tail], axis=1)

    def local(a, o, first, rows):
        total = None
        for h in range(2):
            p = dot(packed(a // 2, h, o // 2, o % 2, first, rows), WE[o % 2, a, h], 1, 0)
            total = p if total is None else total + p
        return total

    def half(dr):
        return pl.ds(HALF * dr, HALF)

    def chain(a, dr, s, rows, sem=None):
        sem = s if sem is None else sem
        start(
            ("chain", a, dr, sem),
            copy(
                sent.at[a, dr, s, rows],
                got.at[a, dr, s, rows],
                rs_s.at[a, dr, sem],
                rs_r.at[a, dr, sem],
                (right, left)[dr],
            ),
        )

    def step0(a):
        for dr in range(2):
            sent[a, dr, 0, half(dr), :] = local(a, PLACE[4], 2 * dr, HALF).astype(BF16)
            chain(a, dr, 0, half(dr))

    def step(a, s):
        for dr in range(2):
            part[dr] = local(a, PLACE[(4 - s, 4 + s)[dr]], 0, BLOCK)
        for dr in range(2):
            arrive("chain", a, dr, s - 1)
            if s == 2:
                arrive("chain", a, dr, 4)
            sent[a, dr, s] = (part[dr] + got[a, dr, s - 1].astype(F32)).astype(BF16)
            chain(a, dr, s, pl.ds(0, BLOCK))

    def step1a(a):
        for dr in range(2):
            ahead[a, dr] = local(a, PLACE[(3, 5)[dr]], 2 * dr, HALF)
            sent[a, dr, 1, half(1 - dr), :] = local(a, PLACE[(3, 5)[dr]], 2 - 2 * dr, HALF).astype(BF16)
            chain(a, dr, 1, half(1 - dr), 4)

    def step1b(a):
        for dr in range(2):
            arrive("chain", a, dr, 0)
            sent[a, dr, 1, half(dr), :] = (ahead[a, dr] + got[a, dr, 0, half(dr), :].astype(F32)).astype(BF16)
            chain(a, dr, 1, half(dr))

    def finish(a):
        final[a] = local(a, PLACE[0], 0, BLOCK)
        for dr in range(2):
            arrive("chain", a, dr, 3)
        final[a] += got[a, 0, 3].astype(F32) + got[a, 1, 3].astype(F32)

    def relay_step(m, s):
        for dr in range(2):
            places = (RIGHTWARD, LEFTWARD)[dr]
            if s > 0:
                arrive("relay", m, dr, s - 1)
            parts = [(s, pl.ds(0, BLOCK))]
            if s == 3 or (s == 2 and m > 0):
                parts = [(s, half(dr)), (4, half(1 - dr))][: 4 - s]
            for sem, rows in parts:
                start(
                    ("relay", m, dr, sem),
                    copy(
                        H.at[m, places[s], rows],
                        H.at[m, places[s + 1], rows],
                        ga_s.at[m, dr, sem],
                        ga_r.at[m, dr, sem],
                        (right, left)[dr],
                    ),
                )

    def relay_rest():
        for m in (1, 2):
            for dr in range(2):
                arrive("relay", m, dr, 4)

    def relay_end(m):
        for dr in range(2):
            arrive("relay", m, dr, 3)

    def activate():
        gate, up = final[0], final[1]
        H[0, PLACE[0]] = ((gate * jax.nn.sigmoid(gate)) * up).astype(BF16)

    def activate_back():
        gate, up, gh = final[0], final[1], final[2]
        sigma = jax.nn.sigmoid(gate)
        H[1, PLACE[0]] = (gh * up * sigma * (1.0 + gate * (1.0 - sigma))).astype(BF16)
        H[2, PLACE[0]] = (gh * (gate * sigma)).astype(BF16)

    def product(i, lo, n):
        def body(o, carry):
            for h in range(2):
                if i == 0:
                    p = dot(H[0, o], WP[2, h], 1, 1)
                else:
                    p = dot(H[1, o], WP[0, h], 1, 1) + dot(H[2, o], WP[1, h], 1, 1)
                S[i, h, o, :, :, pl.ds(0, PIECE), :] = p[:, :LANES].reshape(4, 4, PIECE, LANES)
                tail = p[:, LANES:].reshape(4, 4, PIECE, LANES)
                low = lax.broadcasted_iota(jnp.int32, (4, 4, 8, LANES), 3) < TAIL
                S[i, h, o, :, :, pl.ds(PIECE, 8), :] = jnp.where(low, tail[:, :, :8], tail[:, :, 8:])
            return carry

        if n == 1:
            body(lo, 0)
        else:
            lax.fori_loop(lo, lo + n, body, 0)

    def part_of(i, u):
        cls, lo, n, r, m = PARTS[i][u]
        return cls, lo, n, pl.ds(lo, n), pl.ds(r, m)

    def products(i, g):
        for lo, n in dict.fromkeys(PARTS[i][u][1:3] for u in GROUPS[i][g]):
            product(i, lo, n)
            for u in GROUPS[i][g]:
                if PARTS[i][u][1] == lo:
                    cls, lo, n, span, rows = part_of(i, u)
                    start(
                        ("cores", i, u),
                        copy(
                            S.at[i, other, span, :, :, rows],
                            SR.at[i, span, :, :, rows],
                            sx_s.at[i, u],
                            sx_r.at[i, u],
                            sibling,
                        ),
                    )

    def scatter1(i, g):
        for u in GROUPS[i][g]:
            cls, lo, n, span, rows = part_of(i, u)
            arrive("cores", i, u)
            T[i, span, :, :, rows] = S[i, k, span, :, :, rows] + SR[i, span, :, :, rows]
            for q in (1, 2, 3):
                if cls == 0:
                    src = T.at[i, span, lax.rem(x + q, 4), :, rows]
                else:
                    src = T.at[i, span, :, lax.rem(y + q, 4), rows]
                start(
                    ("scatter", i, u, 0, q),
                    copy(
                        src,
                        RX.at[i, q - 1, span, :, rows],
                        xy_s.at[i, u, 0, q - 1],
                        xy_r.at[i, u, 0, q - 1],
                        peers[cls][q],
                    ),
                )

    def scatter2(i, g):
        for u in GROUPS[i][g]:
            cls, lo, n, span, rows = part_of(i, u)
            total = T[i, span, x, :, rows] if cls == 0 else T[i, span, :, y, rows]
            for q in (1, 2, 3):
                arrive("scatter", i, u, 0, q)
                total = total + RX[i, q - 1, span, :, rows]
            U[i, span, :, rows] = total
            for q in (1, 2, 3):
                at = lax.rem(y + q, 4) if cls == 0 else lax.rem(x + q, 4)
                start(
                    ("scatter", i, u, 1, q),
                    copy(
                        U.at[i, span, at, rows],
                        RY.at[i, q - 1, span, rows],
                        xy_s.at[i, u, 1, q - 1],
                        xy_r.at[i, u, 1, q - 1],
                        peers[1 - cls][q],
                    ),
                )

    def scatter3(i, g):
        for u in GROUPS[i][g]:
            cls, lo, n, span, rows = part_of(i, u)
            total = U[i, span, y if cls == 0 else x, rows]
            for q in (1, 2, 3):
                arrive("scatter", i, u, 1, q)
                total = total + RY[i, q - 1, span, rows]
            for p in range(n):
                rows_out[i, lax.rem(z + ORDER[lo + p], 8), rows, :] = total[p]

    def last_product(step):
        for h in (other, k):
            p = dot(H[1 + step, 0], WP[step, h], 1, 1)
            if step == 0:
                part[h] = p
                continue
            p += part[h]
            S[1, h, 0, :, :, pl.ds(0, PIECE), :] = p[:, :LANES].reshape(4, 4, PIECE, LANES)
            tail = p[:, LANES:].reshape(4, 4, PIECE, LANES)
            low = lax.broadcasted_iota(jnp.int32, (4, 4, 8, LANES), 3) < TAIL
            S[1, h, 0, :, :, pl.ds(PIECE, 8), :] = jnp.where(low, tail[:, :, :8], tail[:, :, 8:])
            if h is other:
                start(("cores", 1, 8), copy(S.at[1, other, 0], SR.at[1, 0], sx_s.at[1, 8], sx_r.at[1, 8], sibling))

    def last1(i, u):
        arrive("cores", i, u)
        T[i, 0] = S[i, k, 0] + SR[i, 0]
        for n, (_, at) in enumerate(plane):
            start(
                ("last", n),
                copy(T.at[i, 0, at // 4, at % 4], RD.at[n], ld_s.at[n], ld_r.at[n], plane[n]),
            )

    def last2(i):
        total = T[i, 0, x, y]
        for n in range(15):
            arrive("last", n)
            total = total + RD[n]
        rows_out[i, lax.rem(z + ORDER[0], 8)] = total

    stores = []

    def store(src, dst):
        c = pltpu.make_async_copy(src, dst, out_s.at[len(stores)])
        c.start()
        stores.append(c)

    def deliver(i):
        one = identity(LANES)
        main = rows_out[i, :, pl.ds(0, PIECE), :].reshape(HALF, LANES)
        tail = rows_out[i, :, pl.ds(PIECE, 8), :]
        tail = jnp.concatenate([tail, tail], axis=1).reshape(HALF, LANES)
        results[i, pl.ds(0, LANES), :] = dot(one, main.astype(BF16), 1, 1).astype(BF16)
        tail = dot(one, tail.astype(BF16), 1, 1)
        low = lax.broadcasted_iota(jnp.int32, (TAIL, HALF), 1) % PIECE < 8
        results[i, pl.ds(LANES, TAIL), :] = jnp.where(low, tail[:TAIL], tail[TAIL:]).astype(BF16)
        store(results.at[i], (out, gt)[i])

    def grad(n, lo, hi):
        a, b = ((0, 1), (0, 2), (1, 0))[n]

        def body(q, carry):
            for h in range(2):
                for e in range(2):
                    p = dot(packed(a, h, q, e, 0, BLOCK), H[b, 2 * q + e], 0, 0)
                    acc[n, h, pl.ds(0, LANES), :] += p[:LANES]
                    acc[n, h, pl.ds(LANES, TAIL), :] += p[LANES + e * TAIL : LANES + (e + 1) * TAIL]
            return carry

        if hi - lo == 1:
            body(lo, 0)
        else:
            lax.fori_loop(lo, hi, body, 0)

    def grad_swap(n):
        gsend[n] = acc[n, other].astype(BF16)
        start(("grad", n), copy(gsend.at[n], ggot.at[n], gr_s.at[n], gr_r.at[n], sibling))
        grads[n, :, mine] = acc[n, k].astype(BF16)

    def grad_end(n):
        arrive("grad", n)
        grads[n, :, theirs] = ggot[n]
        store(grads.at[n], (gg, gu, gd)[n])

    pieces(0)
    piece(0, 0)
    pl.semaphore_wait(barrier, 18)
    direct1(0, 0)
    for q in (1, 2, 3):
        piece(0, q)
    gather1(0, 1)
    swap_weights()
    pieces(1)
    for q in range(4):
        piece(1, q)
    gather1(1, 0)
    gather1(1, 1)
    gather2(0, 1)
    expand_theirs()
    direct2(0, 0)
    acc[...] = jnp.zeros_like(acc)
    gather2(1, 0)
    gather2(1, 1)
    gather1(0, 2)
    gather1(0, 3)
    gather4(0, 0)
    step0(0)
    step0(1)
    gather3(0, 1)
    gather3(1, 0)
    gather4(0, 1)
    step1a(0)
    step1a(1)
    gather2(0, 2)
    gather2(0, 3)
    gather1(1, 2)
    gather1(1, 3)
    step1b(0)
    step1b(1)
    gather4(1, 0)
    step0(2)
    gather3(1, 1)
    gather3(0, 2)
    gather3(0, 3)
    gather2(1, 2)
    gather2(1, 3)
    gather4(0, 2)
    gather4(0, 3)
    step(0, 2)
    step(1, 2)
    gather4(1, 1)
    step1a(2)
    step1b(2)
    gather3(1, 2)
    gather3(1, 3)
    step(0, 3)
    step(1, 3)
    gather4(1, 2)
    gather4(1, 3)
    step(2, 2)
    finish(0)
    finish(1)
    activate()
    relay_step(0, 0)
    step(2, 3)
    relay_step(0, 1)
    finish(2)
    activate_back()
    relay_step(1, 0)
    relay_step(2, 0)
    relay_step(0, 2)
    products(0, 0)
    relay_step(1, 1)
    scatter1(0, 0)
    relay_step(2, 1)
    products(1, 0)
    grad(2, 2, 4)
    relay_step(0, 3)
    products(0, 1)
    scatter1(1, 0)
    scatter2(0, 0)
    relay_step(1, 2)
    scatter1(0, 1)
    relay_step(2, 2)
    products(1, 1)
    scatter2(1, 0)
    relay_end(0)
    products(0, 2)
    scatter1(1, 1)
    grad(2, 0, 2)
    grad_swap(2)
    scatter1(0, 2)
    relay_step(1, 3)
    scatter2(0, 1)
    relay_step(2, 3)
    settle(24)
    relay_rest()
    products(1, 2)
    scatter2(1, 1)
    scatter2(0, 2)
    scatter1(1, 2)
    relay_end(1)
    last_product(0)
    relay_end(2)
    last_product(1)
    grad(0, 0, 4)
    grad_swap(0)
    last1(1, 8)
    scatter2(1, 2)
    grad(1, 0, 4)
    grad_swap(1)
    scatter3(0, 0)
    scatter3(0, 1)
    scatter3(0, 2)
    deliver(0)
    grad_end(2)
    scatter3(1, 0)
    scatter3(1, 1)
    grad_end(0)
    grad_end(1)
    settle(18)
    scatter3(1, 2)
    last2(1)
    deliver(1)
    for c in stores:
        c.wait()
    settle()


def hand_over(*refs):
    held, results, kept, sems = refs[:5], refs[5:10], refs[10:15], refs[15]
    loads = [pltpu.make_async_copy(held[i], kept[i], sems.at[0, i]) for i in range(5)]
    stores = [pltpu.make_async_copy(kept[i], results[i], sems.at[1, i]) for i in range(5)]
    for c in loads:
        c.start()
    for load, store in zip(loads, stores):
        load.wait()
        store.start()
    for c in stores:
        c.wait()


def body(tokens, gate_weight, up_weight, down_weight, cotangent):
    n_tok, width = tokens.shape
    hidden = gate_weight.shape[1]
    dma = pltpu.SemaphoreType.DMA
    V = pltpu.VMEM
    act = jax.ShapeDtypeStruct((width, n_tok), BF16)
    weight = jax.ShapeDtypeStruct((width, hidden), BF16)
    shapes = (act, act, weight, weight, weight)
    scratch = [
        V((2, width, n_tok), BF16),
        V((3, width, hidden), BF16),
        V((2, 2, n_tok, LANES), F32),
        V((2, 2, 4, 4, 4, 3 * PIECE, LANES), BF16),
        V((3, 2, width, BLOCK), BF16),
        V((2, 3, 2, 2 * LANES, BLOCK), BF16),
        V((3, 2, 2 * LANES, BLOCK), BF16),
        V((3, 2, 4, BLOCK, BLOCK), BF16),
        V((3, 2, 4, BLOCK, BLOCK), BF16),
        V((2, BLOCK, BLOCK), F32),
        V((3, 2, HALF, BLOCK), F32),
        V((3, BLOCK, BLOCK), F32),
        V((3, 8, BLOCK, BLOCK), BF16),
        V((2, 2, 8, 4, 4, 24, LANES), F32),
        V((2, 8, 4, 4, 24, LANES), F32),
        V((2, 8, 4, 4, 24, LANES), F32),
        V((2, 3, 8, 4, 24, LANES), F32),
        V((2, 8, 4, 24, LANES), F32),
        V((2, 3, 8, 24, LANES), F32),
        V((15, 24, LANES), F32),
        V((3, 2, width, BLOCK), F32),
        V((3, width, BLOCK), BF16),
        V((3, width, BLOCK), BF16),
        V((3, width, hidden), BF16),
        V((2, 8, 24, LANES), F32),
        V((2, width, n_tok), BF16),
        dma((5,)), dma((5,)),
        dma((3,)), dma((3,)),
        dma((15,)), dma((15,)),
        dma((2, 4, 2, 3)), dma((2, 4, 2, 3)),
        dma((2, 4)), dma((2, 4)),
        dma((3, 2, 5)), dma((3, 2, 5)),
        dma((3, 2, 5)), dma((3, 2, 5)),
        dma((2, 10)), dma((2, 10)),
        dma((2, 10, 2, 3)), dma((2, 10, 2, 3)),
        dma((3,)), dma((3,)),
        dma((15,)), dma((15,)),
    ]
    anywhere = pl.BlockSpec(memory_space=pl.ANY)
    held = pl.pallas_call(
        kernel,
        out_shape=shapes,
        in_specs=[anywhere] * 5,
        out_specs=(anywhere,) * 5,
        scratch_shapes=scratch,
        name="feed_forward",
        compiler_params=pltpu.CompilerParams(
            collective_id=0, has_side_effects=True, vmem_limit_bytes=56 * 2**20
        ),
    )(tokens.T, gate_weight, up_weight, down_weight.T, cotangent.T)
    results = pl.pallas_call(
        hand_over,
        out_shape=shapes,
        in_specs=[anywhere] * 5,
        out_specs=(anywhere,) * 5,
        scratch_shapes=[V(v.shape, BF16) for v in shapes] + [dma((2, 5))],
        name="hand_over",
        compiler_params=pltpu.CompilerParams(vmem_limit_bytes=60 * 2**20),
    )(*held)
    return results[0].T, results[1].T, results[2], results[3], results[4].T


def solution(mesh):
    return jax.shard_map(
        body,
        mesh=mesh,
        in_specs=(
            P("col", "row"),
            P("row", "col"),
            P("row", "col"),
            P("col", "row"),
            P("col", "row"),
        ),
        out_specs=(
            P("col", "row"),
            P("col", "row"),
            P("row", "col"),
            P("row", "col"),
            P("col", "row"),
        ),
        check_vma=False,
    )
```
